128 devices in a mesh: ctx: 16 (over z, x), head: 8 (over y, core).
Axes of the slice: x: 4, y: 4, z: 4, core: 2. Of those that a mesh axis runs over, the one named last changes fastest.
Arguments:
- queries: bfloat16 [8192, 4096], P('ctx', 'head'), may hold values from -48 to 48
- key_rows: bfloat16 [8192, 1024], P('ctx', 'head'), may hold values from -6 to 6
- value_rows: bfloat16 [8192, 1024], P('ctx', 'head'), may hold values from -6 to 6
- b_input: bfloat16 [8192, 2048], P('ctx', 'head'), may hold values from -0.015625 to 0.015625
- c_input: bfloat16 [8192, 2048], P('ctx', 'head'), may hold values from -3 to 3
- step_log: float32 [8192, 32], P('ctx', 'head'), may hold values from -2 to 0, as said below
- doc_lengths: int32 [8], replicated, may hold values from 1 to 4096, 8192 in all
- out_weight: bfloat16 [4096, 4096], P('head'), may hold values from -0.046875 to 0.046875
Outputs:
- projected: float32 [4096, 8192], P('head', 'ctx')
The draws below stay inside these ranges and needn't reach their ends.
Inputs may be any that keep to these rules, and one draw needn't show every extreme that they name: `doc_lengths`: the longest document has exactly 4096 positions; the lengths sum to 8192. `step_log`: negative in every entry.
All inputs are finite; a program needn't handle non-finite values.
Results may differ from the reference program's by a relative error of at most 0.0039.
Values may be sent and summed in bfloat16 or wider, within the bound.
No kernel may reach another device: no remote copies, remote signals or barrier semaphores. Data moves between devices by JAX's collectives and lax.ppermute only.
A program may use at most 64 MiB of HBM per device.

```python
import math
import jax
import jax.numpy as jnp
import numpy as np
from jax import lax

D = 4096
P_SIZE = 128
QUERY_HEADS = 32
KV_HEADS = 8
N = 64
STRETCH = 256
NDOCS = 8
TOK_DEV = 512
PACK_TOKENS = 8192
DOC_MOST = 4096


def draw_key_rows(key, part):
    key = jax.random.fold_in(key, 11)
    base = jnp.clip(jax.random.normal(key, (PACK_TOKENS, KV_HEADS * P_SIZE), jnp.float32), -6.0, 6.0)
    return base.astype(jnp.bfloat16)


def draw_queries(key, part):
    key = jax.random.fold_in(key, 12)
    base = jnp.clip(2.0 * jax.random.normal(key, (PACK_TOKENS, QUERY_HEADS * P_SIZE), jnp.float32), -16.0, 16.0)
    return base.astype(jnp.bfloat16)


def draw_step_log(key, part):
    key = jax.random.fold_in(key, 13)
    selection_key, quick_random_key, gradual_random_key, token_random_key, partition_key, spike_random_key, amount_random_key = jax.random.split(key, 7)
    fast_heads = jax.random.randint(selection_key, (QUERY_HEADS,), 0, 2) == 0
    fast_rate = jnp.exp(jax.random.uniform(quick_random_key, (QUERY_HEADS,), jnp.float32, math.log(1.0 / 50.0), math.log(1.0 / 30.0)))
    slow_rate = jnp.exp(jax.random.uniform(gradual_random_key, (QUERY_HEADS,), jnp.float32, math.log(0.05), math.log(0.5))) / PACK_TOKENS
    rates = jnp.where(fast_heads, fast_rate, slow_rate)
    rough = jnp.exp(jax.random.uniform(token_random_key, (PACK_TOKENS, QUERY_HEADS), jnp.float32, -0.5, 0.5))
    shard_factor = jax.random.uniform(partition_key, (PACK_TOKENS // TOK_DEV, QUERY_HEADS), jnp.float32, 0.5, 2.0)
    shard_factor = jnp.repeat(shard_factor, TOK_DEV, axis=0)
    logarithms = -rates[None, :] * rough * shard_factor
    spike_rows = jax.random.randint(spike_random_key, (4,), 0, PACK_TOKENS)
    spike_amount = jnp.log(jax.random.uniform(amount_random_key, (4, QUERY_HEADS), jnp.float32, 0.5, 0.8))
    return logarithms.at[spike_rows].add(spike_amount)


def levels(own_key, shape, cuts, smallest, largest):
    def one(axis_at, shards_of):
        draws = jax.random.uniform(jax.random.fold_in(jax.random.fold_in(own_key, 6), axis_at), (shards_of,), jnp.float32, smallest / len(cuts), largest / len(cuts))
        return jnp.repeat(jnp.exp(draws), shape[axis_at] // shards_of).reshape((-1,) + (1,) * (len(shape) - axis_at - 1))

    factor_of = one(*cuts[0])
    for cut in cuts[1:]:
        factor_of = factor_of * one(*cut)
    return factor_of


def split_up(amount, total, limit, skew):
    loads = [(1 << 20) // math.isqrt(rank ** skew) + 1 for rank in range(2, amount + 1)]
    surplus, counts = total - limit - (amount - 1), [1] * (amount - 1)
    while surplus > 0:
        candidates = [i for i in range(amount - 1) if counts[i] < limit]
        mass, remaining = sum([loads[i] for i in candidates]), surplus
        for i in candidates:
            extra = min(limit - counts[i], max(1, remaining * loads[i] // mass), surplus)
            counts[i] = counts[i] + extra
            surplus = surplus - extra
    return np.array([limit] + counts)


def ragged_sizes(rng, amount, total, reach, skew):
    if amount == 2:
        one = jax.random.randint(rng, (), max(1, total - reach), min(reach, total - 1) + 1)
        return jnp.stack([one, total - one])
    sizes = jnp.asarray(split_up(amount, total, reach, skew), jnp.int32)
    couples = (amount - 1) // 2
    source_of, sink = sizes[1:1 + 2 * couples:2], sizes[2:2 + 2 * couples:2]
    margin = jnp.minimum(source_of - 1, reach - sink)
    shifted = jax.random.randint(jax.random.fold_in(rng, 1), (couples,), 0, 1 << 20) % (margin + 1)
    sizes = sizes.at[1:1 + 2 * couples:2].set(source_of - shifted).at[2:2 + 2 * couples:2].set(sink + shifted)
    return sizes[jax.random.permutation(jax.random.fold_in(rng, 2), amount)]


def gaussian(own_key, dims, scale, most, cuts=(), held_as=jnp.bfloat16):
    factor_of = levels(own_key, dims, cuts, -0.22, 0.18) if cuts else 1.0
    values = jax.random.normal(own_key, dims, jnp.float32) * scale * factor_of
    return jnp.minimum(jnp.maximum(values, -most), most).astype(held_as)


def setup_inputs(seed: int = 0) -> dict:
    key_list = jax.random.split(jax.random.key(seed), 9)
    queries = draw_queries(jax.random.fold_in(key_list[8], 71), 0)
    key_rows = draw_key_rows(jax.random.fold_in(key_list[8], 71), 0)
    value_rows = gaussian(key_list[2], (PACK_TOKENS, KV_HEADS * P_SIZE), 1.0, 6.0, ((0, 16), (1, 8)))
    b_input = gaussian(key_list[3], (PACK_TOKENS, QUERY_HEADS * N), (N * PACK_TOKENS // 4) ** -0.5, 0.015625, ((0, 16), (1, 8)))
    c_input = gaussian(key_list[4], (PACK_TOKENS, QUERY_HEADS * N), 0.5, 3.0, ((0, 16), (1, 8)))
    step_log = draw_step_log(jax.random.fold_in(key_list[8], 71), 0)
    doc_lengths = ragged_sizes(key_list[6], NDOCS, PACK_TOKENS, DOC_MOST, 2).astype(jnp.int32)
    out_weight = gaussian(key_list[7], (QUERY_HEADS * P_SIZE, D), (4 * QUERY_HEADS * P_SIZE) ** -0.5, 0.046875, ((0, 8),))
    return {"queries": queries, "key_rows": key_rows, "value_rows": value_rows, "b_input": b_input, "c_input": c_input, "step_log": step_log, "doc_lengths": doc_lengths, "out_weight": out_weight}


def doc_index(positions, doc_ends):
    return jnp.sum((positions[:, None] >= doc_ends[None, :]).astype(jnp.int32), axis=1)


def teacher_mix(queries, key_rows, value_rows, doc_ids):
    score_scale = P_SIZE ** -0.5
    repeats = QUERY_HEADS // KV_HEADS
    q_heads = queries.reshape(PACK_TOKENS, QUERY_HEADS, P_SIZE).transpose(1, 0, 2)
    k_heads = jnp.repeat(key_rows.reshape(PACK_TOKENS, KV_HEADS, P_SIZE), repeats, axis=1).transpose(1, 0, 2)
    v_heads = jnp.repeat(value_rows.reshape(PACK_TOKENS, KV_HEADS, P_SIZE), repeats, axis=1).transpose(1, 0, 2)
    q_block = min(PACK_TOKENS, 1024)
    positions = jnp.arange(PACK_TOKENS, dtype=jnp.int32)

    def per_head(inputs):
        q_single, k_single, v_single = inputs

        def per_block(block_index):
            first_row = (block_index * q_block).astype(jnp.int32)
            q_part = lax.dynamic_slice_in_dim(q_single, first_row, q_block, 0)
            q_positions = first_row + jnp.arange(q_block, dtype=jnp.int32)
            q_docs = lax.dynamic_slice_in_dim(doc_ids, first_row, q_block, 0)
            scores = jnp.dot(q_part, k_single.T, preferred_element_type=jnp.float32) * score_scale
            visible = (positions[None, :] <= q_positions[:, None]) & (doc_ids[None, :] == q_docs[:, None])
            row_top = jnp.max(jnp.where(visible, scores, -1e30), axis=1)
            expo = jnp.where(visible, jnp.exp(scores - row_top[:, None]), 0.0)
            totals = jnp.sum(expo, axis=1)
            mixed = jnp.dot(expo.astype(jnp.bfloat16), v_single, preferred_element_type=jnp.float32)
            return mixed / totals[:, None]

        outputs = lax.map(per_block, jnp.arange(PACK_TOKENS // q_block, dtype=jnp.int32))
        return outputs.reshape(PACK_TOKENS, P_SIZE)

    result = lax.map(per_head, (q_heads, k_heads, v_heads))
    return result.transpose(1, 0, 2)


def student_mix(b_input, c_input, value_rows, step_log, doc_ids, doc_ends):
    blocks_all = PACK_TOKENS // STRETCH
    repeats = QUERY_HEADS // KV_HEADS
    cum_log = jnp.cumsum(step_log.reshape(blocks_all, STRETCH, QUERY_HEADS), axis=1)
    block_docs = doc_ids.reshape(blocks_all, STRETCH)
    block_first = jnp.arange(blocks_all, dtype=jnp.int32) * STRETCH
    lead_doc = jnp.where(block_first == 0, -1, doc_index(block_first - 1, doc_ends))
    b_four = b_input.reshape(blocks_all, STRETCH, QUERY_HEADS, N).astype(jnp.float32)
    c_four = c_input.reshape(blocks_all, STRETCH, QUERY_HEADS, N).astype(jnp.float32)
    v_four = jnp.repeat(value_rows.reshape(blocks_all, STRETCH, KV_HEADS, P_SIZE), repeats, axis=2).astype(jnp.float32)
    inner_pos = jnp.arange(STRETCH, dtype=jnp.int32)
    visible = (inner_pos[None, None, :] <= inner_pos[None, :, None]) & (block_docs[:, :, None] == block_docs[:, None, :])
    products = jnp.einsum('cthn,cshn->chts', c_four, b_four)
    log_gap = (cum_log[:, :, None, :] - cum_log[:, None, :, :]).transpose(0, 3, 1, 2)
    decays = jnp.exp(jnp.where(visible[:, None, :, :], log_gap, -jnp.inf))
    mixing = (products * decays).astype(jnp.bfloat16)
    inner = jnp.einsum('chts,cshp->cthp', mixing.astype(jnp.float32), v_four)
    last_doc = block_docs[:, -1]
    keeps = (block_docs == last_doc[:, None])[:, :, None]
    state_weights = jnp.exp(jnp.where(keeps, cum_log[:, -1:, :] - cum_log, -jnp.inf))
    stretch_state = jnp.einsum('cshn,cshp->chnp', b_four * state_weights[..., None], v_four, precision=lax.Precision.HIGHEST)
    carry_factor = jnp.exp(cum_log[:, -1, :]) * (lead_doc == last_doc).astype(jnp.float32)[:, None]

    def advance(running, inputs):
        state_now, factor_now = inputs
        return factor_now[:, None, None] * running + state_now, running

    start_state = jnp.zeros((QUERY_HEADS, N, P_SIZE), jnp.float32)
    final_state, entering = lax.scan(advance, start_state, (stretch_state, carry_factor))
    enter_mask = (block_docs == lead_doc[:, None]).astype(jnp.float32)
    outer = jnp.einsum('cthn,chnp->cthp', c_four, entering, precision=lax.Precision.HIGHEST)
    outer = outer * (jnp.exp(cum_log) * enter_mask[:, :, None])[..., None]
    return (inner + outer).reshape(PACK_TOKENS, QUERY_HEADS, P_SIZE)


def reference(queries, key_rows, value_rows, b_input, c_input, step_log, doc_lengths, out_weight):
    doc_ends = jnp.cumsum(doc_lengths).astype(jnp.int32)
    doc_ids = doc_index(jnp.arange(PACK_TOKENS, dtype=jnp.int32), doc_ends)
    teacher = teacher_mix(queries, key_rows, value_rows, doc_ids)
    student = student_mix(b_input, c_input, value_rows, step_log, doc_ids, doc_ends)
    gap = (student - teacher).reshape(PACK_TOKENS, QUERY_HEADS * P_SIZE).astype(jnp.bfloat16)
    return lax.dot_general(out_weight, gap, (((0,), (1,)), ((), ())), preferred_element_type=jnp.float32)
```

```python
import functools

import jax
import jax.numpy as jnp
from jax import lax
from jax.experimental import pallas as pl
from jax.experimental.pallas import tpu as pltpu
from jax.sharding import PartitionSpec as P

TOK = 512
HEADS = 4
WIDTH = 128
STATE = 64
EXTRA = 16
SCALE = WIDTH**-0.5 * 1.4426950408889634
LOW = -1e30
NT = (((1,), (1,)), ((), ()))
TN = (((0,), (0,)), ((), ()))
F32 = jnp.float32
BF16 = jnp.bfloat16
VMEM = pl.BlockSpec(memory_space=pltpu.VMEM)
SMEM = pl.BlockSpec(memory_space=pltpu.SMEM)


def dot(a, b, dims):
    return lax.dot_general(a, b, dims, preferred_element_type=F32)


def doc_ends(len_ref):
    ends, total = [], jnp.int32(0)
    for d in range(7):
        total = total + len_ref[d]
        ends.append(total)
    return ends


def doc_start(ends, position):
    start = jnp.zeros_like(position)
    for end in ends:
        start = jnp.where(position >= end, end, start)
    return start


def three(value):
    one = value.astype(BF16)
    rest = value - one.astype(F32)
    two = rest.astype(BF16)
    return one, two, (rest - two.astype(F32)).astype(BF16)


def state_kernel(len_ref, b_ref, v_ref, log_ref, st_ref, row_ref, col_ref):
    first = lax.axis_index("ctx") * TOK
    ends = doc_ends(len_ref)
    last_start = doc_start(ends, first + TOK - 1)
    tri = (
        lax.broadcasted_iota(jnp.int32, (TOK, TOK), 0)
        >= lax.broadcasted_iota(jnp.int32, (TOK, TOK), 1)
    ).astype(F32).astype(BF16)
    parts = three(log_ref[...])
    col = sum(dot(tri, part, (((1,), (0,)), ((), ()))) for part in parts[::-1])
    row = sum(dot(part, tri, (((0,), (1,)), ((), ()))) for part in parts[::-1])
    col_ref[...] = jnp.concatenate([col, jnp.zeros((TOK, 128 - HEADS), F32)], axis=1)
    row_ref[...] = jnp.concatenate([row, jnp.zeros((8 - HEADS, TOK), F32)], axis=0)
    final = col[TOK - 1 :, :]
    where_now = first + lax.broadcasted_iota(jnp.int32, (TOK, HEADS), 0)
    weight = jnp.exp(jnp.where(where_now >= last_start, final - col, -jnp.inf))
    lane = lax.broadcasted_iota(jnp.int32, (TOK, 128), 1)
    v = v_ref[...]
    for pair in range(2):
        spread = jnp.where(
            lane < STATE,
            jnp.broadcast_to(weight[:, 2 * pair : 2 * pair + 1], (TOK, 128)),
            jnp.broadcast_to(weight[:, 2 * pair + 1 : 2 * pair + 2], (TOK, 128)),
        )
        scaled = b_ref[:, pl.ds(pair * 128, 128)].astype(F32) * spread
        high = scaled.astype(BF16)
        low = (scaled - high.astype(F32)).astype(BF16)
        st_ref[pl.ds(pair * 128, 128), :] = dot(high, v, TN) + dot(low, v, TN)
    kept = jnp.where(last_start < first, 1.0, 0.0).astype(F32)
    for h in range(HEADS):
        st_ref[pl.ds(256 + 8 * h, 8), :] = jnp.broadcast_to(
            jnp.exp(final[:, h : h + 1]) * kept, (8, 128)
        )


def own_kernel(len_ref, q_ref, kv_ref, b_ref, c_ref, row_ref, col_ref, m_ref, acc_ref, inner_ref):
    first = lax.axis_index("ctx") * TOK
    ends = doc_ends(len_ref)
    query = first + lax.broadcasted_iota(jnp.int32, (1, TOK), 1)
    start = doc_start(ends, query)
    key = first + lax.broadcasted_iota(jnp.int32, (TOK, 1), 0)
    visible = (key >= start) & (key <= query)
    v = kv_ref[:, WIDTH:]
    wide = jnp.concatenate([v, jnp.ones((TOK, EXTRA), BF16)], axis=1)
    lane = lax.broadcasted_iota(jnp.int32, (TOK, 128), 1)

    def score(h):
        return dot(kv_ref[:, :WIDTH], q_ref[:, pl.ds(h * WIDTH, WIDTH)], NT)

    def products(h):
        pair = pl.ds((h // 2) * 128, 128)
        mine = (lane < STATE) if h % 2 == 0 else (lane >= STATE)
        chosen = jnp.where(mine, c_ref[:, pair].astype(F32), 0.0).astype(BF16)
        return dot(b_ref[:, pair], chosen, NT)

    scores = score(0)
    for h in range(HEADS):
        mixed = products(h)
        s = jnp.where(visible, scores * SCALE, LOW)
        top = jnp.max(s, axis=0, keepdims=True)
        p = jnp.exp2(s - top).astype(BF16)
        if h + 1 < HEADS:
            scores = score(h + 1)
        m_ref[h : h + 1, :] = top
        acc_ref[h] = dot(wide, p, TN)
        gap = row_ref[h : h + 1, :] - col_ref[:, h : h + 1]
        mixing = (mixed * jnp.exp(jnp.where(visible, gap, -jnp.inf))).astype(BF16)
        inner_ref[pl.ds(h * WIDTH, WIDTH), :] = dot(v, mixing, TN)
    m_ref[HEADS:, :] = jnp.zeros((8 - HEADS, TOK), F32)


def attend(q_ref, steps, ends, first, m_ref, acc_ref):
    query = first + lax.broadcasted_iota(jnp.int32, (1, TOK), 1)
    start = doc_start(ends, query)
    earliest = doc_start(ends, first)
    latest = doc_start(ends, first + TOK - 1)

    def one(step, masked):
        def part(columns):
            return jnp.concatenate(
                [ref[pl.ds(row, TOK), columns] for ref, row, base in step], axis=0
            )

        rows = TOK * len(step)

        def score(h):
            return dot(part(pl.ds(0, WIDTH)), q_ref[:, pl.ds(h * WIDTH, WIDTH)], NT)

        if masked:
            inside = lax.broadcasted_iota(jnp.int32, (TOK, 1), 0)
            key = jnp.concatenate([base + inside for ref, row, base in step], axis=0)
            visible = key >= start
        wide = jnp.concatenate(
            [part(pl.ds(WIDTH, WIDTH)), jnp.ones((rows, EXTRA), BF16)], axis=1
        )
        scores = score(0)
        for h in range(HEADS):
            s = scores * SCALE
            if h + 1 < HEADS:
                scores = score(h + 1)
            if masked:
                s = jnp.where(visible, s, LOW)
            old = m_ref[h : h + 1, :]
            top = jnp.maximum(old, jnp.max(s, axis=0, keepdims=True))
            p = jnp.exp2(s - top).astype(BF16)
            m_ref[h : h + 1, :] = top
            acc_ref[h] = acc_ref[h] * jnp.exp2(old - top) + dot(wide, p, TN)

    for step in steps:
        highest = functools.reduce(jnp.maximum, [base for ref, row, base in step])
        lowest = functools.reduce(jnp.minimum, [base for ref, row, base in step])
        needed = (highest >= 0) & (highest + TOK > earliest)
        whole = (lowest >= 0) & (lowest >= latest)
        pl.when(needed & whole)(functools.partial(one, step, False))
        pl.when(needed & jnp.logical_not(whole))(functools.partial(one, step, True))


def place():
    ctx = lax.axis_index("ctx")
    x = lax.rem(ctx, 4)
    return ctx, ctx - x, x


def z_kernel(len_ref, q_ref, one_ref, two_ref, mi_ref, ai_ref, m_ref, acc_ref):
    ctx, _, _ = place()
    m_ref[...] = mi_ref[...]
    acc_ref[...] = ai_ref[...]
    step = [(one_ref, 0, (ctx - 4) * TOK), (two_ref, 0, (ctx - 8) * TOK)]
    attend(q_ref, [step], doc_ends(len_ref), ctx * TOK, m_ref, acc_ref)


def bases(row, x, other):
    return jnp.where(other < x, row + other, row - 8 + other) * TOK, (row - 4 + other) * TOK


def near_kernel(len_ref, q_ref, a_ref, b_ref, mi_ref, ai_ref, m_ref, acc_ref):
    ctx, row, x = place()
    m_ref[...] = mi_ref[...]
    acc_ref[...] = ai_ref[...]
    steps = []
    for ref, other in ((a_ref, lax.bitwise_xor(x, 1)), (b_ref, 3 - x)):
        chosen, upper = bases(row, x, other)
        steps.append([(ref, 0, chosen), (ref, TOK, upper)])
    attend(q_ref, steps, doc_ends(len_ref), ctx * TOK, m_ref, acc_ref)


def last_kernel(
    len_ref, q_ref, a_ref, b_ref, mi_ref, ai_ref, c_ref, row_ref, inner_ref, enter_ref, gap_ref, m_ref, acc_ref
):
    ctx, row, x = place()
    first = ctx * TOK
    ends = doc_ends(len_ref)
    m_ref[...] = mi_ref[...]
    acc_ref[...] = ai_ref[...]
    chosen, upper = bases(row, x, lax.bitwise_xor(x, 2))
    attend(q_ref, [[(a_ref, 0, chosen), (b_ref, 0, upper)]], ends, first, m_ref, acc_ref)
    query = first + lax.broadcasted_iota(jnp.int32, (1, TOK), 1)
    enters = doc_start(ends, query) < first
    lane = lax.broadcasted_iota(jnp.int32, (TOK, 128), 1)
    for h in range(HEADS):
        pair = pl.ds((h // 2) * 128, 128)
        mine = (lane < STATE) if h % 2 == 0 else (lane >= STATE)
        chosen = jnp.where(mine, c_ref[:, pair].astype(F32), 0.0).astype(BF16)
        entering = enter_ref[pair, :]
        high = entering.astype(BF16)
        low = (entering - high.astype(F32)).astype(BF16)
        outer = dot(high, chosen, (((0,), (1,)), ((), ()))) + dot(
            low, chosen, (((0,), (1,)), ((), ()))
        )
        gate = jnp.where(enters, jnp.exp(row_ref[h : h + 1, :]), 0.0)
        student = inner_ref[pl.ds(h * WIDTH, WIDTH), :] + outer * gate
        teacher = acc_ref[h, :WIDTH, :] / acc_ref[h, WIDTH : WIDTH + 1, :]
        gap_ref[pl.ds(h * WIDTH, WIDTH), :] = (student - teacher).astype(BF16)


def project_kernel(w_ref, ws_ref, gap_ref, gs_ref, own_ref, up_ref, down_ref, far_ref):
    head = lax.axis_index("head")
    y, core = lax.div(head, 2), lax.rem(head, 2)
    for ref, step in ((far_ref, 2), (up_ref, 1), (down_ref, 3), (own_ref, 0)):
        to = lax.rem(y + step, 4)
        mine = pl.ds(pl.multiple_of((2 * to + core) * TOK, TOK), TOK)
        theirs = pl.ds(pl.multiple_of(to * TOK, TOK), TOK)
        total = dot(w_ref[:, mine], gap_ref[...], TN) + dot(ws_ref[:, theirs], gs_ref[...], TN)
        ref[...] = total.astype(ref.dtype)


def call(body, outs, name, ins, aliases=None, flops=0, scratch=()):
    return pl.pallas_call(
        body,
        out_shape=[jax.ShapeDtypeStruct(shape, kind) for shape, kind in outs],
        in_specs=ins,
        out_specs=[VMEM] * len(outs),
        scratch_shapes=list(scratch),
        compiler_params=pltpu.CompilerParams(vmem_limit_bytes=48 << 20),
        cost_estimate=pl.CostEstimate(flops=flops, bytes_accessed=4 << 20, transcendentals=0),
        name=name,
    )


def within(rows, pairs):
    return [(4 * z + a, 4 * z + b) for z in range(rows) for a, b in pairs]


def local(queries, key_rows, value_rows, b_input, c_input, step_log, lengths, out_weight):
    ctx, head = lax.axis_index("ctx"), lax.axis_index("head")
    x, core = lax.rem(ctx, 4), lax.rem(head, 2)
    even = within(4, [(0, 1), (1, 0), (2, 3), (3, 2)])
    odd = within(4, [(1, 2), (2, 1), (3, 0), (0, 3)])
    far = within(4, [(0, 2), (2, 0), (1, 3), (3, 1)])
    row_1 = [(i, i + 4) for i in range(12)]
    row_2 = [(i, i + 8) for i in range(8)]
    siblings = [(i, i ^ 1) for i in range(8)]

    kv = jnp.concatenate([key_rows, value_rows], axis=1)
    kv_1 = lax.ppermute(kv, "ctx", row_1)
    kv_2 = lax.ppermute(kv, "ctx", row_2)
    for_sibling = lax.dynamic_index_in_dim(
        out_weight.reshape(TOK, 4, 2, TOK), 1 - core, axis=2, keepdims=False
    ).reshape(TOK, 4 * TOK)
    w_sibling = lax.ppermute(for_sibling, "head", siblings)

    state, cum_row, cum_col = call(
        state_kernel,
        [((288, 128), F32), ((8, TOK), F32), ((TOK, 128), F32)],
        "shard_state",
        [SMEM] + [VMEM] * 3,
        flops=2 * TOK * TOK * 128 * 6,
    )(lengths, b_input, value_rows, step_log)

    def split(packed):
        return packed[:256].reshape(HEADS, STATE, WIDTH), packed[256:].reshape(HEADS, 8, WIDTH)

    def pack(value, factor):
        return jnp.concatenate([value.reshape(256, WIDTH), factor.reshape(32, WIDTH)], axis=0)

    def join(earlier, later):
        return later[1][:, :1] * earlier[0] + later[0], earlier[1] * later[1]

    def choose(condition, yes, no):
        return tuple(jnp.where(condition, a, b) for a, b in zip(yes, no))

    mine = split(state)
    other = split(lax.ppermute(state, "ctx", even))
    is_odd, is_high = lax.rem(x, 2) == 1, x >= 2
    pair = join(choose(is_odd, other, mine), choose(is_odd, mine, other))
    none = (jnp.zeros_like(mine[0]), jnp.ones_like(mine[1]))
    before = choose(is_odd, other, none)

    m, acc, inner = call(
        own_kernel,
        [((8, TOK), F32), ((HEADS, WIDTH + EXTRA, TOK), F32), ((TOK, TOK), F32)],
        "own_shard",
        [SMEM] + [VMEM] * 6,
        flops=2 * TOK * TOK * 128 * 4 * 5,
    )(lengths, queries, kv, b_input, c_input, cum_row, cum_col)

    other_pair = split(lax.ppermute(pack(*pair), "ctx", far))
    total = join(choose(is_high, other_pair, pair), choose(is_high, pair, other_pair))
    before = choose(is_high, join(other_pair, before), before)

    send_a = jnp.concatenate([jnp.where(lax.rem(x, 2) == 0, kv, kv_2), kv_1], axis=0)
    send_b = jnp.concatenate([jnp.where(x < 2, kv, kv_2), kv_1], axis=0)
    got_a = lax.ppermute(send_a, "ctx", even)
    got_b = lax.ppermute(send_b, "ctx", odd)

    m, acc = call(
        z_kernel,
        [((8, TOK), F32), ((HEADS, WIDTH + EXTRA, TOK), F32)],
        "same_column",
        [SMEM] + [VMEM] * 5,
        flops=2 * TOK * 1024 * 128 * 4 * 4,
    )(lengths, queries, kv_1, kv_2, m, acc)

    packed_total = pack(*total)
    total_1 = split(lax.ppermute(packed_total, "ctx", row_1))
    total_2 = split(lax.ppermute(packed_total, "ctx", row_2))

    far_a = lax.ppermute(got_b[:TOK], "ctx", even)
    far_b = lax.ppermute(got_a[TOK:], "ctx", odd)

    m, acc = call(
        near_kernel,
        [((8, TOK), F32), ((HEADS, WIDTH + EXTRA, TOK), F32)],
        "near_columns",
        [SMEM] + [VMEM] * 5,
        flops=2 * TOK * 2048 * 128 * 4 * 4,
    )(lengths, queries, got_a, got_b, m, acc)

    row_enter = join(total_2, total_1)
    entering = join(row_enter, before)[0].reshape(256, WIDTH)

    (gap,) = call(
        last_kernel,
        [((TOK, TOK), BF16)],
        "far_column",
        [SMEM] + [VMEM] * 9,
        flops=2 * TOK * 1024 * 128 * 4 * 4,
        scratch=[pltpu.VMEM((8, TOK), F32), pltpu.VMEM((HEADS, WIDTH + EXTRA, TOK), F32)],
    )(lengths, queries, far_a, far_b, m, acc, c_input, cum_row, inner, entering)

    gap_sibling = lax.ppermute(gap, "head", siblings)
    own, up, down, opposite = call(
        project_kernel,
        [((TOK, TOK), F32)] + [((TOK, TOK), BF16)] * 3,
        "project",
        [VMEM] * 4,
        flops=2 * TOK * 1024 * 2048,
    )(out_weight, w_sibling, gap, gap_sibling)

    def line(step):
        return [(2 * y + c, 2 * ((y + step) % 4) + c) for y in range(4) for c in range(2)]

    opposite = lax.ppermute(opposite, "head", line(2))
    up = lax.ppermute(up, "head", line(1))
    down = lax.ppermute(down, "head", line(3))
    return own + up.astype(F32) + down.astype(F32) + opposite.astype(F32)


def solution(mesh):
    split = P("ctx", "head")
    in_specs = (split, split, split, split, split, split, P(), P("head", None))
    return jax.shard_map(
        local, mesh=mesh, in_specs=in_specs, out_specs=P("head", "ctx"), check_vma=False
    )
```

```python
import functools

import jax
import jax.numpy as jnp
from jax import lax
from jax.experimental import pallas as pl
from jax.experimental.pallas import tpu as pltpu
from jax.sharding import PartitionSpec as P

TOK = 512
HEADS = 4
WIDTH = 128
STATE = 64
EXTRA = 16
SCALE = WIDTH**-0.5 * 1.4426950408889634
LOW = -1e30
NT = (((1,), (1,)), ((), ()))
TN = (((0,), (0,)), ((), ()))
F32 = jnp.float32
BF16 = jnp.bfloat16
VMEM = pl.BlockSpec(memory_space=pltpu.VMEM)
SMEM = pl.BlockSpec(memory_space=pltpu.SMEM)
HBM = pl.BlockSpec(memory_space=pltpu.HBM)
PART = 256


def dot(a, b, dims):
    return lax.dot_general(a, b, dims, preferred_element_type=F32)


def doc_ends(len_ref):
    ends, total = [], jnp.int32(0)
    for d in range(7):
        total = total + len_ref[d]
        ends.append(total)
    return ends


def doc_start(ends, position):
    start = jnp.zeros_like(position)
    for end in ends:
        start = jnp.where(position >= end, end, start)
    return start


def three(value):
    one = value.astype(BF16)
    rest = value - one.astype(F32)
    two = rest.astype(BF16)
    return one, two, (rest - two.astype(F32)).astype(BF16)


def begin(pairs, sems, first=0):
    copies = [pltpu.make_async_copy(a, b, sems.at[first + i]) for i, (a, b) in enumerate(pairs)]
    for copy in copies:
        copy.start()
    return copies


def shard_state(first, last_start, b_ref, v, log, st_ref):
    tri = (
        lax.broadcasted_iota(jnp.int32, (TOK, TOK), 0)
        >= lax.broadcasted_iota(jnp.int32, (TOK, TOK), 1)
    ).astype(F32).astype(BF16)
    parts = three(log)
    col = sum(dot(tri, part, NT) for part in parts[::-1])
    row = sum(dot(part, tri, NT) for part in parts[::-1])
    final = col[TOK - 1 :, :]
    where_now = first + lax.broadcasted_iota(jnp.int32, (TOK, HEADS), 0)
    weight = jnp.exp(jnp.where(where_now >= last_start, final - col, -jnp.inf))
    lane = lax.broadcasted_iota(jnp.int32, (TOK, 128), 1)
    for pair in range(2):
        spread = jnp.where(
            lane < STATE,
            jnp.broadcast_to(weight[:, 2 * pair : 2 * pair + 1], (TOK, 128)),
            jnp.broadcast_to(weight[:, 2 * pair + 1 : 2 * pair + 2], (TOK, 128)),
        )
        scaled = b_ref[:, pl.ds(pair * 128, 128)].astype(F32) * spread
        high = scaled.astype(BF16)
        low = (scaled - high.astype(F32)).astype(BF16)
        st_ref[pl.ds(pair * 128, 128), :] = dot(high, v, TN) + dot(low, v, TN)
    kept = jnp.where(last_start < first, 1.0, 0.0).astype(F32)
    for h in range(HEADS):
        st_ref[pl.ds(256 + 8 * h, 8), :] = jnp.broadcast_to(
            jnp.exp(final[:, h : h + 1]) * kept, (8, 128)
        )
    return col, row


def cut_kernel(w_ref, token_ref, send_ref, sems):
    other = 1 - lax.rem(lax.axis_index("head"), 2)
    cuts = []
    for j in range(4):
        source = pl.ds(pl.multiple_of((2 * j + other) * TOK, TOK), TOK)
        cuts.append((w_ref.at[:, source], send_ref.at[:, pl.ds(j * TOK, TOK)]))
    for copy in begin(cuts, sems):
        copy.wait()


def state_kernel(
    len_ref, k_any, v_any, log_any, b_any, kv_ref, st_ref, row_ref, col_ref, b_ref, log_ref, sems
):
    pairs = (
        (k_any, kv_ref.at[:, pl.ds(0, WIDTH)]),
        (v_any, kv_ref.at[:, pl.ds(WIDTH, WIDTH)]),
        (log_any, log_ref),
        (b_any, b_ref),
    )
    for copy in begin(pairs, sems):
        copy.wait()
    first = lax.axis_index("ctx") * TOK
    last_start = doc_start(doc_ends(len_ref), first + TOK - 1)
    col, row = shard_state(first, last_start, b_ref, kv_ref[:, WIDTH:], log_ref[...], st_ref)
    row_ref[...] = jnp.concatenate([row, jnp.zeros((8 - HEADS, TOK), F32)], axis=0)
    col_ref[...] = jnp.concatenate([col, jnp.zeros((TOK, 128 - HEADS), F32)], axis=1)


def own_kernel(
    len_ref,
    row_ref,
    col_ref,
    kv_any,
    b_any,
    q_any,
    c_any,
    m_ref,
    acc_ref,
    inner_ref,
    q_ref,
    c_ref,
    kv_ref,
    b_ref,
    sems,
):
    pairs = ((kv_any, kv_ref), (b_any, b_ref), (q_any, q_ref), (c_any, c_ref))
    for copy in begin(pairs, sems):
        copy.wait()
    first = lax.axis_index("ctx") * TOK
    ends = doc_ends(len_ref)
    v = kv_ref[:, WIDTH:]
    query = first + lax.broadcasted_iota(jnp.int32, (1, TOK), 1)
    start = doc_start(ends, query)
    key = first + lax.broadcasted_iota(jnp.int32, (TOK, 1), 0)
    visible = (key >= start) & (key <= query)
    wide = jnp.concatenate([v, jnp.ones((TOK, EXTRA), BF16)], axis=1)
    lane = lax.broadcasted_iota(jnp.int32, (TOK, 128), 1)

    def score(h):
        return dot(kv_ref[:, :WIDTH], q_ref[:, pl.ds(h * WIDTH, WIDTH)], NT)

    def products(h):
        pair = pl.ds((h // 2) * 128, 128)
        mine = (lane < STATE) if h % 2 == 0 else (lane >= STATE)
        chosen = jnp.where(mine, c_ref[:, pair].astype(F32), 0.0).astype(BF16)
        return dot(b_ref[:, pair], chosen, NT)

    scores = score(0)
    for h in range(HEADS):
        mixed = products(h)
        s = jnp.where(visible, scores * SCALE, LOW)
        top = jnp.max(s, axis=0, keepdims=True)
        p = jnp.exp2(s - top).astype(BF16)
        if h + 1 < HEADS:
            scores = score(h + 1)
        m_ref[h : h + 1, :] = top
        acc_ref[h] = dot(wide, p, TN)
        gap = row_ref[h : h + 1, :] - col_ref[:, h : h + 1]
        mixing = (mixed * jnp.exp(jnp.where(visible, gap, -jnp.inf))).astype(BF16)
        inner_ref[pl.ds(h * WIDTH, WIDTH), :] = dot(v, mixing, TN)
    m_ref[HEADS:, :] = jnp.zeros((8 - HEADS, TOK), F32)


def attend(q_ref, steps, ends, first, offset, width, m_ref, acc_ref):
    query = first + offset + lax.broadcasted_iota(jnp.int32, (1, width), 1)
    start = doc_start(ends, query)
    earliest = doc_start(ends, first + offset)
    latest = doc_start(ends, first + offset + width - 1)

    def one(step, masked):
        def part(columns):
            return jnp.concatenate(
                [ref[pl.ds(row, TOK), columns] for ref, row, base in step], axis=0
            )

        rows = TOK * len(step)

        def score(h):
            q = q_ref[pl.ds(offset, width), pl.ds(h * WIDTH, WIDTH)]
            return dot(part(pl.ds(0, WIDTH)), q, NT)

        if masked:
            inside = lax.broadcasted_iota(jnp.int32, (TOK, 1), 0)
            key = jnp.concatenate([base + inside for ref, row, base in step], axis=0)
            visible = key >= start
        wide = jnp.concatenate(
            [part(pl.ds(WIDTH, WIDTH)), jnp.ones((rows, EXTRA), BF16)], axis=1
        )
        scores = score(0)
        for h in range(HEADS):
            s = scores * SCALE
            if h + 1 < HEADS:
                scores = score(h + 1)
            if masked:
                s = jnp.where(visible, s, LOW)
            old = m_ref[h : h + 1, :]
            top = jnp.maximum(old, jnp.max(s, axis=0, keepdims=True))
            p = jnp.exp2(s - top).astype(BF16)
            m_ref[h : h + 1, :] = top
            acc_ref[h] = acc_ref[h] * jnp.exp2(old - top) + dot(wide, p, TN)

    for step in steps:
        highest = functools.reduce(jnp.maximum, [base for ref, row, base in step])
        lowest = functools.reduce(jnp.minimum, [base for ref, row, base in step])
        needed = (highest >= 0) & (highest + TOK > earliest)
        whole = (lowest >= 0) & (lowest >= latest)
        pl.when(needed & whole)(functools.partial(one, step, False))
        pl.when(needed & jnp.logical_not(whole))(functools.partial(one, step, True))


def place():
    ctx = lax.axis_index("ctx")
    x = lax.rem(ctx, 4)
    return ctx, ctx - x, x


def z_kernel(len_ref, q_ref, one_ref, two_ref, mi_ref, ai_ref, m_ref, acc_ref):
    ctx, _, _ = place()
    step = [(one_ref, 0, (ctx - 4) * TOK), (two_ref, 0, (ctx - 8) * TOK)]
    attend(q_ref, [step], doc_ends(len_ref), ctx * TOK, 0, TOK, m_ref, acc_ref)


def bases(row, x, other):
    return jnp.where(other < x, row + other, row - 8 + other) * TOK, (row - 4 + other) * TOK


def near_kernel(len_ref, q_ref, a_ref, b_ref, mi_ref, ai_ref, m_ref, acc_ref):
    ctx, row, x = place()
    steps = []
    for ref, other in ((a_ref, lax.bitwise_xor(x, 1)), (b_ref, 3 - x)):
        chosen, upper = bases(row, x, other)
        steps.append([(ref, 0, chosen), (ref, TOK, upper)])
    attend(q_ref, steps, doc_ends(len_ref), ctx * TOK, 0, TOK, m_ref, acc_ref)


def last_kernel(
    offset, len_ref, q_ref, a_ref, b_ref, mi_ref, ai_ref, c_ref, row_ref, inner_ref, before_ref, one_ref, two_ref, gap_ref, m_ref, acc_ref
):
    ctx, row, x = place()
    first = ctx * TOK
    ends = doc_ends(len_ref)
    now = pl.ds(offset, PART)
    m_ref[...] = mi_ref[:, now]
    acc_ref[...] = ai_ref[:, :, now]
    chosen, upper = bases(row, x, lax.bitwise_xor(x, 2))
    step = [(a_ref, 0, chosen), (b_ref, 0, upper)]
    attend(q_ref, [step], ends, first, offset, PART, m_ref, acc_ref)
    query = first + offset + lax.broadcasted_iota(jnp.int32, (1, PART), 1)
    enters = doc_start(ends, query) < first
    lane = lax.broadcasted_iota(jnp.int32, (PART, 128), 1)

    def enter(h):
        value, factor = pl.ds(h * STATE, STATE), pl.ds(256 + 8 * h, 1)
        above = jnp.where(ctx >= 8, two_ref[value, :], 0.0)
        above = jnp.where(ctx >= 4, one_ref[value, :] + one_ref[factor, :] * above, 0.0)
        return before_ref[value, :] + before_ref[factor, :] * above

    for h in range(HEADS):
        pair = pl.ds((h // 2) * 128, 128)
        mine = (lane < STATE) if h % 2 == 0 else (lane >= STATE)
        chosen = jnp.where(mine, c_ref[now, pair].astype(F32), 0.0).astype(BF16)
        entering = jnp.concatenate([enter(2 * (h // 2)), enter(2 * (h // 2) + 1)], axis=0)
        high = entering.astype(BF16)
        low = (entering - high.astype(F32)).astype(BF16)
        outer = dot(high, chosen, (((0,), (1,)), ((), ()))) + dot(
            low, chosen, (((0,), (1,)), ((), ()))
        )
        gate = jnp.where(enters, jnp.exp(row_ref[h : h + 1, now]), 0.0)
        student = inner_ref[pl.ds(h * WIDTH, WIDTH), now] + outer * gate
        teacher = acc_ref[h, :WIDTH, :] / acc_ref[h, WIDTH : WIDTH + 1, :]
        gap_ref[pl.ds(h * WIDTH, WIDTH), :] = (student - teacher).astype(BF16)


def project_kernel(w_ref, ws_ref, gap_ref, gs_ref, own_ref, up_ref, down_ref, far_ref):
    head = lax.axis_index("head")
    y, core = lax.div(head, 2), lax.rem(head, 2)
    for ref, step in ((far_ref, 2), (up_ref, 1), (down_ref, 3), (own_ref, 0)):
        to = lax.rem(y + step, 4)
        mine = pl.ds(pl.multiple_of((2 * to + core) * TOK, TOK), TOK)
        theirs = pl.ds(pl.multiple_of(to * TOK, TOK), TOK)
        total = dot(w_ref[:, mine], gap_ref[...], TN) + dot(ws_ref[:, theirs], gs_ref[...], TN)
        ref[...] = total.astype(ref.dtype)


def sum_kernel(part, own_ref, up_ref, down_ref, far_ref, *rest):
    out_ref, total_ref, sems = rest[-3:]
    copies = []
    for i in range(4):
        rows = pl.ds(i * 128, 128)
        total = own_ref[rows, :] + up_ref[rows, :].astype(F32)
        total_ref[rows, :] = total + (down_ref[rows, :].astype(F32) + far_ref[rows, :].astype(F32))
        to = out_ref.at[rows, pl.ds(part * PART, PART)]
        copies.append(pltpu.make_async_copy(total_ref.at[rows, :], to, sems.at[i]))
        copies[-1].start()
    for copy in copies:
        copy.wait()


def call(body, outs, name, ins, aliases=None, flops=0, scratch=(), out_specs=None, limit=24):
    return pl.pallas_call(
        body,
        out_shape=[jax.ShapeDtypeStruct(shape, kind) for shape, kind in outs],
        in_specs=ins,
        out_specs=out_specs or [VMEM] * len(outs),
        scratch_shapes=list(scratch),
        input_output_aliases=aliases or {},
        compiler_params=pltpu.CompilerParams(vmem_limit_bytes=limit << 20),
        cost_estimate=pl.CostEstimate(flops=flops, bytes_accessed=1024, transcendentals=0),
        name=name,
    )


def sums(part, arrays, before):
    more = [] if before is None else [before]
    (result,) = call(
        functools.partial(sum_kernel, part),
        [((TOK, TOK), F32)],
        "sum_part",
        [VMEM] * 4 + [HBM] * len(more),
        aliases={4: 0} if more else None,
        flops=1024,
        scratch=[pltpu.VMEM((TOK, PART), F32), pltpu.SemaphoreType.DMA((4,))],
        out_specs=[HBM],
    )(*arrays, *more)
    return result


def within(rows, pairs):
    return [(4 * z + a, 4 * z + b) for z in range(rows) for a, b in pairs]


def local(queries, key_rows, value_rows, b_input, c_input, step_log, lengths, out_weight):
    ctx = lax.axis_index("ctx")
    x = lax.rem(ctx, 4)
    even = within(4, [(0, 1), (1, 0), (2, 3), (3, 2)])
    odd = within(4, [(1, 2), (2, 1), (3, 0), (0, 3)])
    far = within(4, [(0, 2), (2, 0), (1, 3), (3, 1)])
    row_1 = [(i, (i + 4) % 16) for i in range(16)]
    row_2 = [(i, (i + 8) % 16) for i in range(16)]
    siblings = [(i, i ^ 1) for i in range(8)]

    sem = pltpu.SemaphoreType.DMA
    kv, state, cum_row, cum_col = call(
        state_kernel,
        [((TOK, 256), BF16), ((288, 128), F32), ((8, TOK), F32), ((TOK, 128), F32)],
        "shard_state",
        [SMEM] + [HBM] * 4,
        flops=2 << 30,
        scratch=[pltpu.VMEM((TOK, 256), BF16), pltpu.VMEM((HEADS, TOK), F32), sem((4,))],
        limit=54,
    )(lengths, key_rows, value_rows, step_log.T, b_input)
    kv_1 = lax.ppermute(kv, "ctx", row_1)
    kv_2 = lax.ppermute(kv, "ctx", row_2)
    m, acc, inner, q, c = call(
        own_kernel,
        [
            ((8, TOK), F32),
            ((HEADS, WIDTH + EXTRA, TOK), F32),
            ((TOK, TOK), F32),
            ((TOK, TOK), BF16),
            ((TOK, 256), BF16),
        ],
        "own_shard",
        [SMEM] + [VMEM] * 2 + [HBM] * 4,
        flops=6 << 30,
        scratch=[pltpu.VMEM((TOK, 256), BF16), pltpu.VMEM((TOK, 256), BF16), sem((4,))],
        limit=54,
    )(lengths, cum_row, cum_col, kv, b_input, queries, c_input)
    def split(packed):
        return packed[:256].reshape(HEADS, STATE, WIDTH), packed[256:].reshape(HEADS, 8, WIDTH)

    def pack(value, factor):
        return jnp.concatenate([value.reshape(256, WIDTH), factor.reshape(32, WIDTH)], axis=0)

    def join(earlier, later):
        return later[1][:, :1] * earlier[0] + later[0], earlier[1] * later[1]

    def choose(condition, yes, no):
        return tuple(jnp.where(condition, a, b) for a, b in zip(yes, no))

    mine = split(state)
    other = split(lax.ppermute(state, "ctx", even))
    is_odd, is_high = lax.rem(x, 2) == 1, x >= 2
    pair = join(choose(is_odd, other, mine), choose(is_odd, mine, other))
    none = (jnp.zeros_like(mine[0]), jnp.ones_like(mine[1]))
    before = choose(is_odd, other, none)

    other_pair = split(lax.ppermute(pack(*pair), "ctx", far))
    total = join(choose(is_high, other_pair, pair), choose(is_high, pair, other_pair))
    before = choose(is_high, join(other_pair, before), before)

    send_a = jnp.concatenate([jnp.where(lax.rem(x, 2) == 0, kv, kv_2), kv_1], axis=0)
    send_b = jnp.concatenate([jnp.where(x < 2, kv, kv_2), kv_1], axis=0)
    got_a = lax.ppermute(send_a, "ctx", even)
    got_b = lax.ppermute(send_b, "ctx", odd)

    m, acc = call(
        z_kernel,
        [((8, TOK), F32), ((HEADS, WIDTH + EXTRA, TOK), F32)],
        "same_column",
        [SMEM] + [VMEM] * 5,
        aliases={4: 0, 5: 1},
        flops=4 << 30,
    )(lengths, q, kv_1, kv_2, m, acc)

    packed_total = pack(*total)
    (for_sibling,) = call(
        cut_kernel,
        [((TOK, 4 * TOK), BF16)],
        "cut_weight",
        [VMEM] * 2,
        scratch=[sem((4,))],
        flops=2 << 30,
    )(out_weight, packed_total[:8])
    w_sibling = lax.ppermute(for_sibling, "head", siblings)
    total_1 = lax.ppermute(packed_total, "ctx", row_1)
    total_2 = lax.ppermute(packed_total, "ctx", row_2)
    before = pack(*before)

    far_a = lax.ppermute(got_b[:TOK], "ctx", even)
    far_b = lax.ppermute(got_a[TOK:], "ctx", odd)

    m, acc = call(
        near_kernel,
        [((8, TOK), F32), ((HEADS, WIDTH + EXTRA, TOK), F32)],
        "near_columns",
        [SMEM] + [VMEM] * 5,
        aliases={4: 0, 5: 1},
        flops=7 << 30,
    )(lengths, q, got_a, got_b, m, acc)

    def line(step):
        return [(2 * y + c, 2 * ((y + step) % 4) + c) for y in range(4) for c in range(2)]

    result = None
    for part in range(TOK // PART):
        (gap,) = call(
            functools.partial(last_kernel, part * PART),
            [((TOK, PART), BF16)],
            "far_column",
            [SMEM] + [VMEM] * 11,
            flops=5 << 29,
            scratch=[pltpu.VMEM((8, PART), F32), pltpu.VMEM((HEADS, WIDTH + EXTRA, PART), F32)],
        )(lengths, q, far_a, far_b, m, acc, c, cum_row, inner, before, total_1, total_2)
        gap_sibling = lax.ppermute(gap, "head", siblings)
        own, up, down, opposite = call(
            project_kernel,
            [((TOK, PART), F32)] + [((TOK, PART), BF16)] * 3,
            "project",
            [VMEM] * 4,
            flops=3 << 29,
        )(out_weight, w_sibling, gap, gap_sibling)
        opposite = lax.ppermute(opposite, "head", line(2))
        up = lax.ppermute(up, "head", line(1))
        down = lax.ppermute(down, "head", line(3))
        result = sums(part, (own, up, down, opposite), result)
    return result


def solution(mesh):
    split = P("ctx", "head")
    in_specs = (split, split, split, split, split, split, P(), P("head", None))
    return jax.shard_map(
        local, mesh=mesh, in_specs=in_specs, out_specs=P("head", "ctx"), check_vma=False
    )
```

```python
import functools

import jax
import jax.numpy as jnp
from jax import lax
from jax.experimental import pallas as pl
from jax.experimental.pallas import tpu as pltpu
from jax.sharding import PartitionSpec as P

TOK = 512
HEADS = 4
WIDTH = 128
STATE = 64
EXTRA = 16
SCALE = WIDTH**-0.5 * 1.4426950408889634
LOW = -1e30
NT = (((1,), (1,)), ((), ()))
TN = (((0,), (0,)), ((), ()))
F32 = jnp.float32
BF16 = jnp.bfloat16
VMEM = pl.BlockSpec(memory_space=pltpu.VMEM)
SMEM = pl.BlockSpec(memory_space=pltpu.SMEM)
HBM = pl.BlockSpec(memory_space=pltpu.HBM)
PART = 256


def dot(a, b, dims):
    return lax.dot_general(a, b, dims, preferred_element_type=F32)


def doc_ends(len_ref):
    ends, total = [], jnp.int32(0)
    for d in range(7):
        total = total + len_ref[d]
        ends.append(total)
    return ends


def doc_start(ends, position):
    start = jnp.zeros_like(position)
    for end in ends:
        start = jnp.where(position >= end, end, start)
    return start


def three(value):
    one = value.astype(BF16)
    rest = value - one.astype(F32)
    two = rest.astype(BF16)
    return one, two, (rest - two.astype(F32)).astype(BF16)


def begin(pairs, sems, first=0):
    copies = [pltpu.make_async_copy(a, b, sems.at[first + i]) for i, (a, b) in enumerate(pairs)]
    for copy in copies:
        copy.start()
    return copies


def shard_state(first, last_start, b_ref, v, log, st_ref):
    tri = (
        lax.broadcasted_iota(jnp.int32, (TOK, TOK), 0)
        >= lax.broadcasted_iota(jnp.int32, (TOK, TOK), 1)
    ).astype(F32).astype(BF16)
    parts = three(log)
    col = sum(dot(tri, part, NT) for part in parts[::-1])
    row = sum(dot(part, tri, NT) for part in parts[::-1])
    final = col[TOK - 1 :, :]
    where_now = first + lax.broadcasted_iota(jnp.int32, (TOK, HEADS), 0)
    weight = jnp.exp(jnp.where(where_now >= last_start, final - col, -jnp.inf))
    lane = lax.broadcasted_iota(jnp.int32, (TOK, 128), 1)
    for pair in range(2):
        spread = jnp.where(
            lane < STATE,
            jnp.broadcast_to(weight[:, 2 * pair : 2 * pair + 1], (TOK, 128)),
            jnp.broadcast_to(weight[:, 2 * pair + 1 : 2 * pair + 2], (TOK, 128)),
        )
        scaled = b_ref[:, pl.ds(pair * 128, 128)].astype(F32) * spread
        high = scaled.astype(BF16)
        low = (scaled - high.astype(F32)).astype(BF16)
        st_ref[pl.ds(pair * 128, 128), :] = dot(high, v, TN) + dot(low, v, TN)
    kept = jnp.where(last_start < first, 1.0, 0.0).astype(F32)
    for h in range(HEADS):
        st_ref[pl.ds(256 + 8 * h, 8), :] = jnp.broadcast_to(
            jnp.exp(final[:, h : h + 1]) * kept, (8, 128)
        )
    return col, row


def state_kernel(
    len_ref, k_any, v_any, log_any, b_any, kv_ref, st_ref, row_ref, col_ref, b_ref, log_ref, sems
):
    pairs = (
        (k_any, kv_ref.at[:, pl.ds(0, WIDTH)]),
        (v_any, kv_ref.at[:, pl.ds(WIDTH, WIDTH)]),
        (log_any, log_ref),
        (b_any, b_ref),
    )
    for copy in begin(pairs, sems):
        copy.wait()
    first = lax.axis_index("ctx") * TOK
    last_start = doc_start(doc_ends(len_ref), first + TOK - 1)
    col, row = shard_state(first, last_start, b_ref, kv_ref[:, WIDTH:], log_ref[...], st_ref)
    row_ref[...] = jnp.concatenate([row, jnp.zeros((8 - HEADS, TOK), F32)], axis=0)
    col_ref[...] = jnp.concatenate([col, jnp.zeros((TOK, 128 - HEADS), F32)], axis=1)


def own_kernel(
    len_ref,
    row_ref,
    col_ref,
    kv_any,
    b_any,
    q_any,
    c_any,
    w_any,
    m_ref,
    acc_ref,
    inner_ref,
    q_ref,
    c_ref,
    send_ref,
    kv_ref,
    b_ref,
    w_ref,
    sems,
):
    pairs = ((kv_any, kv_ref), (b_any, b_ref), (q_any, q_ref), (c_any, c_ref))
    for copy in begin(pairs, sems):
        copy.wait()
    other = 1 - lax.rem(lax.axis_index("head"), 2)
    loads, cuts = [], []
    for j in range(4):
        rows = pl.ds(j * 128, 128)
        loads.append((w_any.at[rows, :], w_ref.at[rows, :]))
        source = pl.ds(pl.multiple_of((2 * j + other) * TOK, TOK), TOK)
        cuts.append((w_ref.at[:, source], send_ref.at[:, pl.ds(j * TOK, TOK)]))
    loads = begin(loads, sems, 4)
    first = lax.axis_index("ctx") * TOK
    ends = doc_ends(len_ref)
    v = kv_ref[:, WIDTH:]
    query = first + lax.broadcasted_iota(jnp.int32, (1, TOK), 1)
    start = doc_start(ends, query)
    key = first + lax.broadcasted_iota(jnp.int32, (TOK, 1), 0)
    visible = (key >= start) & (key <= query)
    wide = jnp.concatenate([v, jnp.ones((TOK, EXTRA), BF16)], axis=1)
    lane = lax.broadcasted_iota(jnp.int32, (TOK, 128), 1)

    def score(h):
        return dot(kv_ref[:, :WIDTH], q_ref[:, pl.ds(h * WIDTH, WIDTH)], NT)

    def products(h):
        pair = pl.ds((h // 2) * 128, 128)
        mine = (lane < STATE) if h % 2 == 0 else (lane >= STATE)
        chosen = jnp.where(mine, c_ref[:, pair].astype(F32), 0.0).astype(BF16)
        return dot(b_ref[:, pair], chosen, NT)

    scores = score(0)
    for h in range(HEADS):
        if h == 3:
            for copy in loads:
                copy.wait()
            cuts = begin(cuts, sems, 8)
        mixed = products(h)
        s = jnp.where(visible, scores * SCALE, LOW)
        top = jnp.max(s, axis=0, keepdims=True)
        p = jnp.exp2(s - top).astype(BF16)
        if h + 1 < HEADS:
            scores = score(h + 1)
        m_ref[h : h + 1, :] = top
        acc_ref[h] = dot(wide, p, TN)
        gap = row_ref[h : h + 1, :] - col_ref[:, h : h + 1]
        mixing = (mixed * jnp.exp(jnp.where(visible, gap, -jnp.inf))).astype(BF16)
        inner_ref[pl.ds(h * WIDTH, WIDTH), :] = dot(v, mixing, TN)
    m_ref[HEADS:, :] = jnp.zeros((8 - HEADS, TOK), F32)
    for copy in cuts:
        copy.wait()


def attend(q_ref, steps, ends, first, offset, width, m_ref, acc_ref):
    query = first + offset + lax.broadcasted_iota(jnp.int32, (1, width), 1)
    start = doc_start(ends, query)
    earliest = doc_start(ends, first + offset)
    latest = doc_start(ends, first + offset + width - 1)

    def one(step, masked):
        def part(columns):
            return jnp.concatenate(
                [ref[pl.ds(row, TOK), columns] for ref, row, base in step], axis=0
            )

        rows = TOK * len(step)

        def score(h):
            q = q_ref[pl.ds(offset, width), pl.ds(h * WIDTH, WIDTH)]
            return dot(part(pl.ds(0, WIDTH)), q, NT)

        if masked:
            inside = lax.broadcasted_iota(jnp.int32, (TOK, 1), 0)
            key = jnp.concatenate([base + inside for ref, row, base in step], axis=0)
            visible = key >= start
        wide = jnp.concatenate(
            [part(pl.ds(WIDTH, WIDTH)), jnp.ones((rows, EXTRA), BF16)], axis=1
        )
        scores = score(0)
        for h in range(HEADS):
            s = scores * SCALE
            if h + 1 < HEADS:
                scores = score(h + 1)
            if masked:
                s = jnp.where(visible, s, LOW)
            old = m_ref[h : h + 1, :]
            top = jnp.maximum(old, jnp.max(s, axis=0, keepdims=True))
            p = jnp.exp2(s - top).astype(BF16)
            m_ref[h : h + 1, :] = top
            acc_ref[h] = acc_ref[h] * jnp.exp2(old - top) + dot(wide, p, TN)

    for step in steps:
        highest = functools.reduce(jnp.maximum, [base for ref, row, base in step])
        lowest = functools.reduce(jnp.minimum, [base for ref, row, base in step])
        needed = (highest >= 0) & (highest + TOK > earliest)
        whole = (lowest >= 0) & (lowest >= latest)
        pl.when(needed & whole)(functools.partial(one, step, False))
        pl.when(needed & jnp.logical_not(whole))(functools.partial(one, step, True))


def place():
    ctx = lax.axis_index("ctx")
    x = lax.rem(ctx, 4)
    return ctx, ctx - x, x


def z_kernel(len_ref, q_ref, one_ref, two_ref, mi_ref, ai_ref, m_ref, acc_ref):
    ctx, _, _ = place()
    step = [(one_ref, 0, (ctx - 4) * TOK), (two_ref, 0, (ctx - 8) * TOK)]
    attend(q_ref, [step], doc_ends(len_ref), ctx * TOK, 0, TOK, m_ref, acc_ref)


def bases(row, x, other):
    return jnp.where(other < x, row + other, row - 8 + other) * TOK, (row - 4 + other) * TOK


def near_kernel(len_ref, q_ref, a_ref, b_ref, mi_ref, ai_ref, m_ref, acc_ref):
    ctx, row, x = place()
    steps = []
    for ref, other in ((a_ref, lax.bitwise_xor(x, 1)), (b_ref, 3 - x)):
        chosen, upper = bases(row, x, other)
        steps.append([(ref, 0, chosen), (ref, TOK, upper)])
    attend(q_ref, steps, doc_ends(len_ref), ctx * TOK, 0, TOK, m_ref, acc_ref)


def last_kernel(
    offset, len_ref, q_ref, a_ref, b_ref, mi_ref, ai_ref, c_ref, row_ref, inner_ref, before_ref, one_ref, two_ref, gap_ref, m_ref, acc_ref
):
    ctx, row, x = place()
    first = ctx * TOK
    ends = doc_ends(len_ref)
    now = pl.ds(offset, PART)
    m_ref[...] = mi_ref[:, now]
    acc_ref[...] = ai_ref[:, :, now]
    chosen, upper = bases(row, x, lax.bitwise_xor(x, 2))
    step = [(a_ref, 0, chosen), (b_ref, 0, upper)]
    attend(q_ref, [step], ends, first, offset, PART, m_ref, acc_ref)
    query = first + offset + lax.broadcasted_iota(jnp.int32, (1, PART), 1)
    enters = doc_start(ends, query) < first
    lane = lax.broadcasted_iota(jnp.int32, (PART, 128), 1)

    def enter(h):
        value, factor = pl.ds(h * STATE, STATE), pl.ds(256 + 8 * h, 1)
        above = jnp.where(ctx >= 8, two_ref[value, :], 0.0)
        above = jnp.where(ctx >= 4, one_ref[value, :] + one_ref[factor, :] * above, 0.0)
        return before_ref[value, :] + before_ref[factor, :] * above

    for h in range(HEADS):
        pair = pl.ds((h // 2) * 128, 128)
        mine = (lane < STATE) if h % 2 == 0 else (lane >= STATE)
        chosen = jnp.where(mine, c_ref[now, pair].astype(F32), 0.0).astype(BF16)
        entering = jnp.concatenate([enter(2 * (h // 2)), enter(2 * (h // 2) + 1)], axis=0)
        high = entering.astype(BF16)
        low = (entering - high.astype(F32)).astype(BF16)
        outer = dot(high, chosen, (((0,), (1,)), ((), ()))) + dot(
            low, chosen, (((0,), (1,)), ((), ()))
        )
        gate = jnp.where(enters, jnp.exp(row_ref[h : h + 1, now]), 0.0)
        student = inner_ref[pl.ds(h * WIDTH, WIDTH), now] + outer * gate
        teacher = acc_ref[h, :WIDTH, :] / acc_ref[h, WIDTH : WIDTH + 1, :]
        gap_ref[pl.ds(h * WIDTH, WIDTH), :] = (student - teacher).astype(BF16)


def project_kernel(w_ref, ws_ref, gap_ref, gs_ref, own_ref, up_ref, down_ref, far_ref):
    head = lax.axis_index("head")
    y, core = lax.div(head, 2), lax.rem(head, 2)
    for ref, step in ((far_ref, 2), (up_ref, 1), (down_ref, 3), (own_ref, 0)):
        to = lax.rem(y + step, 4)
        mine = pl.ds(pl.multiple_of((2 * to + core) * TOK, TOK), TOK)
        theirs = pl.ds(pl.multiple_of(to * TOK, TOK), TOK)
        total = dot(w_ref[:, mine], gap_ref[...], TN) + dot(ws_ref[:, theirs], gs_ref[...], TN)
        ref[...] = total.astype(ref.dtype)


def sum_kernel(part, own_ref, up_ref, down_ref, far_ref, *rest):
    out_ref, total_ref, sems = rest[-3:]
    copies = []
    for i in range(4):
        rows = pl.ds(i * 128, 128)
        total = own_ref[rows, :] + up_ref[rows, :].astype(F32)
        total_ref[rows, :] = total + (down_ref[rows, :].astype(F32) + far_ref[rows, :].astype(F32))
        to = out_ref.at[rows, pl.ds(part * PART, PART)]
        copies.append(pltpu.make_async_copy(total_ref.at[rows, :], to, sems.at[i]))
        copies[-1].start()
    for copy in copies:
        copy.wait()


def call(body, outs, name, ins, aliases=None, flops=0, scratch=(), out_specs=None, limit=24):
    return pl.pallas_call(
        body,
        out_shape=[jax.ShapeDtypeStruct(shape, kind) for shape, kind in outs],
        in_specs=ins,
        out_specs=out_specs or [VMEM] * len(outs),
        scratch_shapes=list(scratch),
        input_output_aliases=aliases or {},
        compiler_params=pltpu.CompilerParams(vmem_limit_bytes=limit << 20),
        cost_estimate=pl.CostEstimate(flops=flops, bytes_accessed=1024, transcendentals=0),
        name=name,
    )


def sums(part, arrays, before):
    more = [] if before is None else [before]
    (result,) = call(
        functools.partial(sum_kernel, part),
        [((TOK, TOK), F32)],
        "sum_part",
        [VMEM] * 4 + [HBM] * len(more),
        aliases={4: 0} if more else None,
        flops=1024,
        scratch=[pltpu.VMEM((TOK, PART), F32), pltpu.SemaphoreType.DMA((4,))],
        out_specs=[HBM],
    )(*arrays, *more)
    return result


def within(rows, pairs):
    return [(4 * z + a, 4 * z + b) for z in range(rows) for a, b in pairs]


def local(queries, key_rows, value_rows, b_input, c_input, step_log, lengths, out_weight):
    ctx = lax.axis_index("ctx")
    x = lax.rem(ctx, 4)
    even = within(4, [(0, 1), (1, 0), (2, 3), (3, 2)])
    odd = within(4, [(1, 2), (2, 1), (3, 0), (0, 3)])
    far = within(4, [(0, 2), (2, 0), (1, 3), (3, 1)])
    row_1 = [(i, (i + 4) % 16) for i in range(16)]
    row_2 = [(i, (i + 8) % 16) for i in range(16)]
    siblings = [(i, i ^ 1) for i in range(8)]

    sem = pltpu.SemaphoreType.DMA
    kv, state, cum_row, cum_col = call(
        state_kernel,
        [((TOK, 256), BF16), ((288, 128), F32), ((8, TOK), F32), ((TOK, 128), F32)],
        "shard_state",
        [SMEM] + [HBM] * 4,
        flops=2 << 30,
        scratch=[pltpu.VMEM((TOK, 256), BF16), pltpu.VMEM((HEADS, TOK), F32), sem((4,))],
        limit=54,
    )(lengths, key_rows, value_rows, step_log.T, b_input)
    kv_1 = lax.ppermute(kv, "ctx", row_1)
    kv_2 = lax.ppermute(kv, "ctx", row_2)
    m, acc, inner, q, c, for_sibling = call(
        own_kernel,
        [
            ((8, TOK), F32),
            ((HEADS, WIDTH + EXTRA, TOK), F32),
            ((TOK, TOK), F32),
            ((TOK, TOK), BF16),
            ((TOK, 256), BF16),
            ((TOK, 4 * TOK), BF16),
        ],
        "own_shard",
        [SMEM] + [VMEM] * 2 + [HBM] * 5,
        flops=6 << 30,
        scratch=[pltpu.VMEM((TOK, 256), BF16), pltpu.VMEM((TOK, 256), BF16), pltpu.VMEM((TOK, 8 * TOK), BF16), sem((12,))],
        out_specs=[VMEM] * 5 + [HBM],
        limit=54,
    )(lengths, cum_row, cum_col, kv, b_input, queries, c_input, out_weight)
    def split(packed):
        return packed[:256].reshape(HEADS, STATE, WIDTH), packed[256:].reshape(HEADS, 8, WIDTH)

    def pack(value, factor):
        return jnp.concatenate([value.reshape(256, WIDTH), factor.reshape(32, WIDTH)], axis=0)

    def join(earlier, later):
        return later[1][:, :1] * earlier[0] + later[0], earlier[1] * later[1]

    def choose(condition, yes, no):
        return tuple(jnp.where(condition, a, b) for a, b in zip(yes, no))

    mine = split(state)
    other = split(lax.ppermute(state, "ctx", even))
    is_odd, is_high = lax.rem(x, 2) == 1, x >= 2
    pair = join(choose(is_odd, other, mine), choose(is_odd, mine, other))
    none = (jnp.zeros_like(mine[0]), jnp.ones_like(mine[1]))
    before = choose(is_odd, other, none)

    other_pair = split(lax.ppermute(pack(*pair), "ctx", far))
    total = join(choose(is_high, other_pair, pair), choose(is_high, pair, other_pair))
    before = choose(is_high, join(other_pair, before), before)

    send_a = jnp.concatenate([jnp.where(lax.rem(x, 2) == 0, kv, kv_2), kv_1], axis=0)
    send_b = jnp.concatenate([jnp.where(x < 2, kv, kv_2), kv_1], axis=0)
    got_a = lax.ppermute(send_a, "ctx", even)
    got_b = lax.ppermute(send_b, "ctx", odd)

    m, acc = call(
        z_kernel,
        [((8, TOK), F32), ((HEADS, WIDTH + EXTRA, TOK), F32)],
        "same_column",
        [SMEM] + [VMEM] * 5,
        aliases={4: 0, 5: 1},
        flops=4 << 30,
    )(lengths, q, kv_1, kv_2, m, acc)

    packed_total = pack(*total)
    w_sibling = lax.ppermute(for_sibling, "head", siblings)
    total_1 = lax.ppermute(packed_total, "ctx", row_1)
    total_2 = lax.ppermute(packed_total, "ctx", row_2)
    before = pack(*before)

    far_a = lax.ppermute(got_b[:TOK], "ctx", even)
    far_b = lax.ppermute(got_a[TOK:], "ctx", odd)

    m, acc = call(
        near_kernel,
        [((8, TOK), F32), ((HEADS, WIDTH + EXTRA, TOK), F32)],
        "near_columns",
        [SMEM] + [VMEM] * 5,
        aliases={4: 0, 5: 1},
        flops=7 << 30,
    )(lengths, q, got_a, got_b, m, acc)

    def line(step):
        return [(2 * y + c, 2 * ((y + step) % 4) + c) for y in range(4) for c in range(2)]

    result = None
    for part in range(TOK // PART):
        (gap,) = call(
            functools.partial(last_kernel, part * PART),
            [((TOK, PART), BF16)],
            "far_column",
            [SMEM] + [VMEM] * 11,
            flops=5 << 29,
            scratch=[pltpu.VMEM((8, PART), F32), pltpu.VMEM((HEADS, WIDTH + EXTRA, PART), F32)],
        )(lengths, q, far_a, far_b, m, acc, c, cum_row, inner, before, total_1, total_2)
        gap_sibling = lax.ppermute(gap, "head", siblings)
        own, up, down, opposite = call(
            project_kernel,
            [((TOK, PART), F32)] + [((TOK, PART), BF16)] * 3,
            "project",
            [VMEM] * 4,
            flops=3 << 29,
        )(out_weight, w_sibling, gap, gap_sibling)
        opposite = lax.ppermute(opposite, "head", line(2))
        up = lax.ppermute(up, "head", line(1))
        down = lax.ppermute(down, "head", line(3))
        result = sums(part, (own, up, down, opposite), result)
    return result


def solution(mesh):
    split = P("ctx", "head")
    in_specs = (split, split, split, split, split, split, P(), P("head", None))
    return jax.shard_map(
        local, mesh=mesh, in_specs=in_specs, out_specs=P("head", "ctx"), check_vma=False
    )
```

```python
import functools

import jax
import jax.numpy as jnp
from jax import lax
from jax.experimental import pallas as pl
from jax.experimental.pallas import tpu as pltpu
from jax.sharding import PartitionSpec as P

TOK = 512
HEADS = 4
WIDTH = 128
STATE = 64
EXTRA = 16
SCALE = WIDTH**-0.5 * 1.4426950408889634
LOW = -1e30
NT = (((1,), (1,)), ((), ()))
TN = (((0,), (0,)), ((), ()))
F32 = jnp.float32
BF16 = jnp.bfloat16
VMEM = pl.BlockSpec(memory_space=pltpu.VMEM)
SMEM = pl.BlockSpec(memory_space=pltpu.SMEM)
HBM = pl.BlockSpec(memory_space=pltpu.HBM)
PART = 256


def dot(a, b, dims):
    return lax.dot_general(a, b, dims, preferred_element_type=F32)


def doc_ends(len_ref):
    ends, total = [], jnp.int32(0)
    for d in range(7):
        total = total + len_ref[d]
        ends.append(total)
    return ends


def doc_start(ends, position):
    start = jnp.zeros_like(position)
    for end in ends:
        start = jnp.where(position >= end, end, start)
    return start


def three(value):
    one = value.astype(BF16)
    rest = value - one.astype(F32)
    two = rest.astype(BF16)
    return one, two, (rest - two.astype(F32)).astype(BF16)


def begin(pairs, sems, first=0):
    copies = [pltpu.make_async_copy(a, b, sems.at[first + i]) for i, (a, b) in enumerate(pairs)]
    for copy in copies:
        copy.start()
    return copies


def shard_state(first, last_start, b_ref, v, log, st_ref):
    tri = (
        lax.broadcasted_iota(jnp.int32, (TOK, TOK), 0)
        >= lax.broadcasted_iota(jnp.int32, (TOK, TOK), 1)
    ).astype(F32).astype(BF16)
    parts = three(log)
    col = sum(dot(tri, part, NT) for part in parts[::-1])
    row = sum(dot(part, tri, NT) for part in parts[::-1])
    final = col[TOK - 1 :, :]
    where_now = first + lax.broadcasted_iota(jnp.int32, (TOK, HEADS), 0)
    weight = jnp.exp(jnp.where(where_now >= last_start, final - col, -jnp.inf))
    lane = lax.broadcasted_iota(jnp.int32, (TOK, 128), 1)
    for pair in range(2):
        spread = jnp.where(
            lane < STATE,
            jnp.broadcast_to(weight[:, 2 * pair : 2 * pair + 1], (TOK, 128)),
            jnp.broadcast_to(weight[:, 2 * pair + 1 : 2 * pair + 2], (TOK, 128)),
        )
        scaled = b_ref[:, pl.ds(pair * 128, 128)].astype(F32) * spread
        high = scaled.astype(BF16)
        low = (scaled - high.astype(F32)).astype(BF16)
        st_ref[pl.ds(pair * 128, 128), :] = dot(high, v, TN) + dot(low, v, TN)
    kept = jnp.where(last_start < first, 1.0, 0.0).astype(F32)
    for h in range(HEADS):
        st_ref[pl.ds(256 + 8 * h, 8), :] = jnp.broadcast_to(
            jnp.exp(final[:, h : h + 1]) * kept, (8, 128)
        )
    return col, row


def state_kernel(
    len_ref, k_any, v_any, log_any, b_any, kv_ref, st_ref, row_ref, col_ref, b_ref, log_ref, sems
):
    pairs = (
        (k_any, kv_ref.at[:, pl.ds(0, WIDTH)]),
        (v_any, kv_ref.at[:, pl.ds(WIDTH, WIDTH)]),
        (log_any, log_ref),
        (b_any, b_ref),
    )
    for copy in begin(pairs, sems):
        copy.wait()
    first = lax.axis_index("ctx") * TOK
    last_start = doc_start(doc_ends(len_ref), first + TOK - 1)
    col, row = shard_state(first, last_start, b_ref, kv_ref[:, WIDTH:], log_ref[...], st_ref)
    row_ref[...] = jnp.concatenate([row, jnp.zeros((8 - HEADS, TOK), F32)], axis=0)
    col_ref[...] = jnp.concatenate([col, jnp.zeros((TOK, 128 - HEADS), F32)], axis=1)


def own_kernel(
    len_ref,
    row_ref,
    col_ref,
    kv_any,
    b_any,
    q_any,
    c_any,
    w_any,
    m_ref,
    acc_ref,
    inner_ref,
    q_ref,
    c_ref,
    send_ref,
    kv_ref,
    b_ref,
    w_ref,
    sems,
):
    pairs = ((kv_any, kv_ref), (b_any, b_ref), (q_any, q_ref), (c_any, c_ref))
    for copy in begin(pairs, sems):
        copy.wait()
    other = 1 - lax.rem(lax.axis_index("head"), 2)
    loads, cuts = [], []
    for j in range(4):
        rows = pl.ds(j * 128, 128)
        loads.append((w_any.at[rows, :], w_ref.at[rows, :]))
        source = pl.ds(pl.multiple_of((2 * j + other) * TOK, TOK), TOK)
        cuts.append((w_ref.at[:, source], send_ref.at[:, pl.ds(j * TOK, TOK)]))
    loads = begin(loads, sems, 4)
    first = lax.axis_index("ctx") * TOK
    ends = doc_ends(len_ref)
    v = kv_ref[:, WIDTH:]
    query = first + lax.broadcasted_iota(jnp.int32, (1, TOK), 1)
    start = doc_start(ends, query)
    key = first + lax.broadcasted_iota(jnp.int32, (TOK, 1), 0)
    visible = (key >= start) & (key <= query)
    wide = jnp.concatenate([v, jnp.ones((TOK, EXTRA), BF16)], axis=1)
    lane = lax.broadcasted_iota(jnp.int32, (TOK, 128), 1)

    def score(h):
        return dot(kv_ref[:, :WIDTH], q_ref[:, pl.ds(h * WIDTH, WIDTH)], NT)

    def products(h):
        pair = pl.ds((h // 2) * 128, 128)
        mine = (lane < STATE) if h % 2 == 0 else (lane >= STATE)
        chosen = jnp.where(mine, c_ref[:, pair].astype(F32), 0.0).astype(BF16)
        return dot(b_ref[:, pair], chosen, NT)

    scores = score(0)
    for h in range(HEADS):
        if h == 3:
            for copy in loads:
                copy.wait()
            cuts = begin(cuts, sems, 8)
        mixed = products(h)
        s = jnp.where(visible, scores * SCALE, LOW)
        top = jnp.max(s, axis=0, keepdims=True)
        p = jnp.exp2(s - top).astype(BF16)
        if h + 1 < HEADS:
            scores = score(h + 1)
        m_ref[h : h + 1, :] = top
        acc_ref[h] = dot(wide, p, TN)
        gap = row_ref[h : h + 1, :] - col_ref[:, h : h + 1]
        mixing = (mixed * jnp.exp(jnp.where(visible, gap, -jnp.inf))).astype(BF16)
        inner_ref[pl.ds(h * WIDTH, WIDTH), :] = dot(v, mixing, TN)
    m_ref[HEADS:, :] = jnp.zeros((8 - HEADS, TOK), F32)
    for copy in cuts:
        copy.wait()


def attend(q_ref, steps, ends, first, offset, width, m_ref, acc_ref):
    query = first + offset + lax.broadcasted_iota(jnp.int32, (1, width), 1)
    start = doc_start(ends, query)
    earliest = doc_start(ends, first + offset)
    latest = doc_start(ends, first + offset + width - 1)

    def one(step, masked):
        def part(columns):
            return jnp.concatenate(
                [ref[pl.ds(row, TOK), columns] for ref, row, base in step], axis=0
            )

        rows = TOK * len(step)

        def score(h):
            q = q_ref[pl.ds(offset, width), pl.ds(h * WIDTH, WIDTH)]
            return dot(part(pl.ds(0, WIDTH)), q, NT)

        if masked:
            inside = lax.broadcasted_iota(jnp.int32, (TOK, 1), 0)
            key = jnp.concatenate([base + inside for ref, row, base in step], axis=0)
            visible = key >= start
        wide = jnp.concatenate(
            [part(pl.ds(WIDTH, WIDTH)), jnp.ones((rows, EXTRA), BF16)], axis=1
        )
        scores = score(0)
        for h in range(HEADS):
            s = scores * SCALE
            if h + 1 < HEADS:
                scores = score(h + 1)
            if masked:
                s = jnp.where(visible, s, LOW)
            old = m_ref[h : h + 1, :]
            top = jnp.maximum(old, jnp.max(s, axis=0, keepdims=True))
            p = jnp.exp2(s - top).astype(BF16)
            m_ref[h : h + 1, :] = top
            acc_ref[h] = acc_ref[h] * jnp.exp2(old - top) + dot(wide, p, TN)

    for step in steps:
        highest = functools.reduce(jnp.maximum, [base for ref, row, base in step])
        lowest = functools.reduce(jnp.minimum, [base for ref, row, base in step])
        needed = (highest >= 0) & (highest + TOK > earliest)
        whole = (lowest >= 0) & (lowest >= latest)
        pl.when(needed & whole)(functools.partial(one, step, False))
        pl.when(needed & jnp.logical_not(whole))(functools.partial(one, step, True))


def place():
    ctx = lax.axis_index("ctx")
    x = lax.rem(ctx, 4)
    return ctx, ctx - x, x


def z_kernel(len_ref, q_ref, one_ref, two_ref, mi_ref, ai_ref, m_ref, acc_ref):
    ctx, _, _ = place()
    step = [(one_ref, 0, (ctx - 4) * TOK), (two_ref, 0, (ctx - 8) * TOK)]
    attend(q_ref, [step], doc_ends(len_ref), ctx * TOK, 0, TOK, m_ref, acc_ref)


def bases(row, x, other):
    return jnp.where(other < x, row + other, row - 8 + other) * TOK, (row - 4 + other) * TOK


def near_kernel(len_ref, q_ref, a_ref, b_ref, mi_ref, ai_ref, m_ref, acc_ref):
    ctx, row, x = place()
    steps = []
    for ref, other in ((a_ref, lax.bitwise_xor(x, 1)), (b_ref, 3 - x)):
        chosen, upper = bases(row, x, other)
        steps.append([(ref, 0, chosen), (ref, TOK, upper)])
    attend(q_ref, steps, doc_ends(len_ref), ctx * TOK, 0, TOK, m_ref, acc_ref)


def last_kernel(
    offset, len_ref, q_ref, a_ref, b_ref, mi_ref, ai_ref, c_ref, row_ref, inner_ref, before_ref, one_ref, two_ref, gap_ref, m_ref, acc_ref
):
    ctx, row, x = place()
    first = ctx * TOK
    ends = doc_ends(len_ref)
    now = pl.ds(offset, PART)
    m_ref[...] = mi_ref[:, now]
    acc_ref[...] = ai_ref[:, :, now]
    chosen, upper = bases(row, x, lax.bitwise_xor(x, 2))
    step = [(a_ref, 0, chosen), (b_ref, 0, upper)]
    attend(q_ref, [step], ends, first, offset, PART, m_ref, acc_ref)
    query = first + offset + lax.broadcasted_iota(jnp.int32, (1, PART), 1)
    enters = doc_start(ends, query) < first
    lane = lax.broadcasted_iota(jnp.int32, (PART, 128), 1)

    def enter(h):
        value, factor = pl.ds(h * STATE, STATE), pl.ds(256 + 8 * h, 1)
        above = jnp.where(ctx >= 8, two_ref[value, :], 0.0)
        above = jnp.where(ctx >= 4, one_ref[value, :] + one_ref[factor, :] * above, 0.0)
        return before_ref[value, :] + before_ref[factor, :] * above

    for h in range(HEADS):
        pair = pl.ds((h // 2) * 128, 128)
        mine = (lane < STATE) if h % 2 == 0 else (lane >= STATE)
        chosen = jnp.where(mine, c_ref[now, pair].astype(F32), 0.0).astype(BF16)
        entering = jnp.concatenate([enter(2 * (h // 2)), enter(2 * (h // 2) + 1)], axis=0)
        high = entering.astype(BF16)
        low = (entering - high.astype(F32)).astype(BF16)
        outer = dot(high, chosen, (((0,), (1,)), ((), ()))) + dot(
            low, chosen, (((0,), (1,)), ((), ()))
        )
        gate = jnp.where(enters, jnp.exp(row_ref[h : h + 1, now]), 0.0)
        student = inner_ref[pl.ds(h * WIDTH, WIDTH), now] + outer * gate
        teacher = acc_ref[h, :WIDTH, :] / acc_ref[h, WIDTH : WIDTH + 1, :]
        gap_ref[pl.ds(h * WIDTH, WIDTH), :] = (student - teacher).astype(BF16)


def project_kernel(w_ref, ws_ref, gap_ref, gs_ref, own_ref, up_ref, down_ref, far_ref):
    head = lax.axis_index("head")
    y, core = lax.div(head, 2), lax.rem(head, 2)
    for ref, step in ((far_ref, 2), (up_ref, 1), (down_ref, 3), (own_ref, 0)):
        to = lax.rem(y + step, 4)
        mine = pl.ds(pl.multiple_of((2 * to + core) * TOK, TOK), TOK)
        theirs = pl.ds(pl.multiple_of(to * TOK, TOK), TOK)
        total = dot(w_ref[:, mine], gap_ref[...], TN) + dot(ws_ref[:, theirs], gs_ref[...], TN)
        ref[...] = total.astype(ref.dtype)


def sum_kernel(*refs):
    out_ref, total_ref, sems = refs[-3:]
    copies = []
    for i in range(4):
        rows = pl.ds(i * 128, 128)
        for part in range(TOK // PART):
            own, up, down, far = (ref[rows, :].astype(F32) for ref in refs[4 * part : 4 * part + 4])
            total_ref[rows, pl.ds(part * PART, PART)] = (own + up) + (down + far)
        copies.append(
            pltpu.make_async_copy(total_ref.at[rows, :], out_ref.at[rows, :], sems.at[i])
        )
        copies[-1].start()
    for copy in copies:
        copy.wait()


def call(body, outs, name, ins, aliases=None, flops=0, scratch=(), out_specs=None, limit=24):
    return pl.pallas_call(
        body,
        out_shape=[jax.ShapeDtypeStruct(shape, kind) for shape, kind in outs],
        in_specs=ins,
        out_specs=out_specs or [VMEM] * len(outs),
        scratch_shapes=list(scratch),
        input_output_aliases=aliases or {},
        compiler_params=pltpu.CompilerParams(vmem_limit_bytes=limit << 20),
        cost_estimate=pl.CostEstimate(flops=flops, bytes_accessed=1024, transcendentals=0),
        name=name,
    )


def within(rows, pairs):
    return [(4 * z + a, 4 * z + b) for z in range(rows) for a, b in pairs]


def local(queries, key_rows, value_rows, b_input, c_input, step_log, lengths, out_weight):
    ctx = lax.axis_index("ctx")
    x = lax.rem(ctx, 4)
    even = within(4, [(0, 1), (1, 0), (2, 3), (3, 2)])
    odd = within(4, [(1, 2), (2, 1), (3, 0), (0, 3)])
    far = within(4, [(0, 2), (2, 0), (1, 3), (3, 1)])
    row_1 = [(i, (i + 4) % 16) for i in range(16)]
    row_2 = [(i, (i + 8) % 16) for i in range(16)]
    siblings = [(i, i ^ 1) for i in range(8)]

    sem = pltpu.SemaphoreType.DMA
    kv, state, cum_row, cum_col = call(
        state_kernel,
        [((TOK, 256), BF16), ((288, 128), F32), ((8, TOK), F32), ((TOK, 128), F32)],
        "shard_state",
        [SMEM] + [HBM] * 4,
        flops=2 << 30,
        scratch=[pltpu.VMEM((TOK, 256), BF16), pltpu.VMEM((HEADS, TOK), F32), sem((4,))],
        limit=54,
    )(lengths, key_rows, value_rows, step_log.T, b_input)
    kv_1 = lax.ppermute(kv, "ctx", row_1)
    kv_2 = lax.ppermute(kv, "ctx", row_2)
    m, acc, inner, q, c, for_sibling = call(
        own_kernel,
        [
            ((8, TOK), F32),
            ((HEADS, WIDTH + EXTRA, TOK), F32),
            ((TOK, TOK), F32),
            ((TOK, TOK), BF16),
            ((TOK, 256), BF16),
            ((TOK, 4 * TOK), BF16),
        ],
        "own_shard",
        [SMEM] + [VMEM] * 2 + [HBM] * 5,
        flops=6 << 30,
        scratch=[pltpu.VMEM((TOK, 256), BF16), pltpu.VMEM((TOK, 256), BF16), pltpu.VMEM((TOK, 8 * TOK), BF16), sem((12,))],
        out_specs=[VMEM] * 5 + [HBM],
        limit=54,
    )(lengths, cum_row, cum_col, kv, b_input, queries, c_input, out_weight)
    def split(packed):
        return packed[:256].reshape(HEADS, STATE, WIDTH), packed[256:].reshape(HEADS, 8, WIDTH)

    def pack(value, factor):
        return jnp.concatenate([value.reshape(256, WIDTH), factor.reshape(32, WIDTH)], axis=0)

    def join(earlier, later):
        return later[1][:, :1] * earlier[0] + later[0], earlier[1] * later[1]

    def choose(condition, yes, no):
        return tuple(jnp.where(condition, a, b) for a, b in zip(yes, no))

    mine = split(state)
    other = split(lax.ppermute(state, "ctx", even))
    is_odd, is_high = lax.rem(x, 2) == 1, x >= 2
    pair = join(choose(is_odd, other, mine), choose(is_odd, mine, other))
    none = (jnp.zeros_like(mine[0]), jnp.ones_like(mine[1]))
    before = choose(is_odd, other, none)

    other_pair = split(lax.ppermute(pack(*pair), "ctx", far))
    total = join(choose(is_high, other_pair, pair), choose(is_high, pair, other_pair))
    before = choose(is_high, join(other_pair, before), before)

    send_a = jnp.concatenate([jnp.where(lax.rem(x, 2) == 0, kv, kv_2), kv_1], axis=0)
    send_b = jnp.concatenate([jnp.where(x < 2, kv, kv_2), kv_1], axis=0)
    got_a = lax.ppermute(send_a, "ctx", even)
    got_b = lax.ppermute(send_b, "ctx", odd)

    m, acc = call(
        z_kernel,
        [((8, TOK), F32), ((HEADS, WIDTH + EXTRA, TOK), F32)],
        "same_column",
        [SMEM] + [VMEM] * 5,
        aliases={4: 0, 5: 1},
        flops=4 << 30,
    )(lengths, q, kv_1, kv_2, m, acc)

    packed_total = pack(*total)
    w_sibling = lax.ppermute(for_sibling, "head", siblings)
    total_1 = lax.ppermute(packed_total, "ctx", row_1)
    total_2 = lax.ppermute(packed_total, "ctx", row_2)
    before = pack(*before)

    far_a = lax.ppermute(got_b[:TOK], "ctx", even)
    far_b = lax.ppermute(got_a[TOK:], "ctx", odd)

    m, acc = call(
        near_kernel,
        [((8, TOK), F32), ((HEADS, WIDTH + EXTRA, TOK), F32)],
        "near_columns",
        [SMEM] + [VMEM] * 5,
        aliases={4: 0, 5: 1},
        flops=7 << 30,
    )(lengths, q, got_a, got_b, m, acc)

    def line(step):
        return [(2 * y + c, 2 * ((y + step) % 4) + c) for y in range(4) for c in range(2)]

    pieces = []
    for part in range(TOK // PART):
        (gap,) = call(
            functools.partial(last_kernel, part * PART),
            [((TOK, PART), BF16)],
            "far_column",
            [SMEM] + [VMEM] * 11,
            flops=5 << 29,
            scratch=[pltpu.VMEM((8, PART), F32), pltpu.VMEM((HEADS, WIDTH + EXTRA, PART), F32)],
        )(lengths, q, far_a, far_b, m, acc, c, cum_row, inner, before, total_1, total_2)
        gap_sibling = lax.ppermute(gap, "head", siblings)
        own, up, down, opposite = call(
            project_kernel,
            [((TOK, PART), F32)] + [((TOK, PART), BF16)] * 3,
            "project",
            [VMEM] * 4,
            flops=3 << 29,
        )(out_weight, w_sibling, gap, gap_sibling)
        opposite = lax.ppermute(opposite, "head", line(2))
        up = lax.ppermute(up, "head", line(1))
        down = lax.ppermute(down, "head", line(3))
        pieces += [own, up, down, opposite]
    (result,) = call(
        sum_kernel,
        [((TOK, TOK), F32)],
        "sum_line",
        [VMEM] * len(pieces),
        flops=1024,
        scratch=[pltpu.VMEM((TOK, TOK), F32), pltpu.SemaphoreType.DMA((4,))],
        out_specs=[HBM],
    )(*pieces)
    return result


def solution(mesh):
    split = P("ctx", "head")
    in_specs = (split, split, split, split, split, split, P(), P("head", None))
    return jax.shard_map(
        local, mesh=mesh, in_specs=in_specs, out_specs=P("head", "ctx"), check_vma=False
    )
```

```python
import functools

import jax
import jax.numpy as jnp
from jax import lax
from jax.experimental import pallas as pl
from jax.experimental.pallas import tpu as pltpu
from jax.sharding import PartitionSpec as P

TOK = 512
HEADS = 4
WIDTH = 128
STATE = 64
EXTRA = 16
SCALE = WIDTH**-0.5 * 1.4426950408889634
LOW = -1e30
NT = (((1,), (1,)), ((), ()))
TN = (((0,), (0,)), ((), ()))
F32 = jnp.float32
BF16 = jnp.bfloat16
VMEM = pl.BlockSpec(memory_space=pltpu.VMEM)
SMEM = pl.BlockSpec(memory_space=pltpu.SMEM)
HBM = pl.BlockSpec(memory_space=pltpu.HBM)
PART = 256


def dot(a, b, dims):
    return lax.dot_general(a, b, dims, preferred_element_type=F32)


def doc_ends(len_ref):
    ends, total = [], jnp.int32(0)
    for d in range(7):
        total = total + len_ref[d]
        ends.append(total)
    return ends


def doc_start(ends, position):
    start = jnp.zeros_like(position)
    for end in ends:
        start = jnp.where(position >= end, end, start)
    return start


def three(value):
    one = value.astype(BF16)
    rest = value - one.astype(F32)
    two = rest.astype(BF16)
    return one, two, (rest - two.astype(F32)).astype(BF16)


def begin(pairs, sems, first=0):
    copies = [pltpu.make_async_copy(a, b, sems.at[first + i]) for i, (a, b) in enumerate(pairs)]
    for copy in copies:
        copy.start()
    return copies


def running_sums(log):
    tri = (
        lax.broadcasted_iota(jnp.int32, (TOK, TOK), 0)
        >= lax.broadcasted_iota(jnp.int32, (TOK, TOK), 1)
    ).astype(F32).astype(BF16)
    parts = three(log)
    col = sum(dot(tri, part, NT) for part in parts[::-1])
    row = sum(dot(part, tri, NT) for part in parts[::-1])
    return col, row


def shard_state(first, last_start, b_ref, v, col, st_ref):
    final = col[TOK - 1 :, :]
    where_now = first + lax.broadcasted_iota(jnp.int32, (TOK, HEADS), 0)
    weight = jnp.exp(jnp.where(where_now >= last_start, final - col, -jnp.inf))
    lane = lax.broadcasted_iota(jnp.int32, (TOK, 128), 1)
    for pair in range(2):
        spread = jnp.where(
            lane < STATE,
            jnp.broadcast_to(weight[:, 2 * pair : 2 * pair + 1], (TOK, 128)),
            jnp.broadcast_to(weight[:, 2 * pair + 1 : 2 * pair + 2], (TOK, 128)),
        )
        scaled = b_ref[:, pl.ds(pair * 128, 128)].astype(F32) * spread
        high = scaled.astype(BF16)
        low = (scaled - high.astype(F32)).astype(BF16)
        st_ref[pl.ds(pair * 128, 128), :] = dot(high, v, TN) + dot(low, v, TN)
    kept = jnp.where(last_start < first, 1.0, 0.0).astype(F32)
    for h in range(HEADS):
        st_ref[pl.ds(256 + 8 * h, 8), :] = jnp.broadcast_to(
            jnp.exp(final[:, h : h + 1]) * kept, (8, 128)
        )


def state_kernel(
    len_ref, k_any, v_any, log_any, b_any, kv_ref, st_ref, row_ref, col_ref, b_ref, log_ref, sems
):
    pairs = (
        (log_any, log_ref),
        (v_any, kv_ref.at[:, pl.ds(WIDTH, WIDTH)]),
        (b_any, b_ref),
        (k_any, kv_ref.at[:, pl.ds(0, WIDTH)]),
    )
    logs, values, inputs, keys = begin(pairs, sems)
    logs.wait()
    col, row = running_sums(log_ref[...])
    for copy in (values, inputs, keys):
        copy.wait()
    first = lax.axis_index("ctx") * TOK
    last_start = doc_start(doc_ends(len_ref), first + TOK - 1)
    shard_state(first, last_start, b_ref, kv_ref[:, WIDTH:], col, st_ref)
    row_ref[...] = jnp.concatenate([row, jnp.zeros((8 - HEADS, TOK), F32)], axis=0)
    col_ref[...] = jnp.concatenate([col, jnp.zeros((TOK, 128 - HEADS), F32)], axis=1)


def own_kernel(
    len_ref,
    row_ref,
    col_ref,
    kv_any,
    b_any,
    q_any,
    c_any,
    w_any,
    m_ref,
    acc_ref,
    inner_ref,
    q_ref,
    c_ref,
    send_ref,
    kv_ref,
    b_ref,
    w_ref,
    sems,
):
    pairs = ((q_any, q_ref), (kv_any, kv_ref), (b_any, b_ref), (c_any, c_ref))
    for copy in begin(pairs, sems):
        copy.wait()
    other = 1 - lax.rem(lax.axis_index("head"), 2)
    loads, cuts = [], []
    for j in range(4):
        rows = pl.ds(j * 128, 128)
        loads.append((w_any.at[rows, :], w_ref.at[rows, :]))
        source = pl.ds(pl.multiple_of((2 * j + other) * TOK, TOK), TOK)
        cuts.append((w_ref.at[:, source], send_ref.at[:, pl.ds(j * TOK, TOK)]))
    loads = begin(loads, sems, 4)
    first = lax.axis_index("ctx") * TOK
    ends = doc_ends(len_ref)
    v = kv_ref[:, WIDTH:]
    query = first + lax.broadcasted_iota(jnp.int32, (1, TOK), 1)
    start = doc_start(ends, query)
    key = first + lax.broadcasted_iota(jnp.int32, (TOK, 1), 0)
    v = kv_ref[:, WIDTH:]
    wide = jnp.concatenate([v, jnp.ones((TOK, EXTRA), BF16)], axis=1)
    lane = lax.broadcasted_iota(jnp.int32, (PART, 128), 1)
    units = [(h, half) for h in range(HEADS) for half in range(TOK // PART)]

    def score(h, half):
        q = q_ref[pl.ds(half * PART, PART), pl.ds(h * WIDTH, WIDTH)]
        return dot(kv_ref[pl.ds(0, (half + 1) * PART), :WIDTH], q, NT)

    def products(h, half):
        pair = pl.ds((h // 2) * 128, 128)
        mine = (lane < STATE) if h % 2 == 0 else (lane >= STATE)
        c = c_ref[pl.ds(half * PART, PART), pair].astype(F32)
        chosen = jnp.where(mine, c, 0.0).astype(BF16)
        return dot(b_ref[pl.ds(0, (half + 1) * PART), pair], chosen, NT)

    scores = score(*units[0])
    for i, (h, half) in enumerate(units):
        if h == 3 and half == 0:
            for copy in loads:
                copy.wait()
            cuts = begin(cuts, sems, 8)
        now, until = pl.ds(half * PART, PART), (half + 1) * PART
        columns = slice(half * PART, until)
        visible = (key[:until] >= start[:, columns]) & (key[:until] <= query[:, columns])
        mixed = products(h, half)
        s = jnp.where(visible, scores * SCALE, LOW)
        top = jnp.max(s, axis=0, keepdims=True)
        p = jnp.exp2(s - top).astype(BF16)
        if i + 1 < len(units):
            scores = score(*units[i + 1])
        m_ref[h : h + 1, now] = top
        acc_ref[h, :, now] = dot(wide[:until], p, TN)
        gap = row_ref[h : h + 1, now] - col_ref[pl.ds(0, until), h : h + 1]
        mixing = (mixed * jnp.exp(jnp.where(visible, gap, -jnp.inf))).astype(BF16)
        inner_ref[pl.ds(h * WIDTH, WIDTH), now] = dot(v[:until], mixing, TN)
    m_ref[HEADS:, :] = jnp.zeros((8 - HEADS, TOK), F32)
    for copy in cuts:
        copy.wait()


def attend(q_ref, steps, ends, first, offset, width, m_ref, acc_ref):
    query = first + offset + lax.broadcasted_iota(jnp.int32, (1, width), 1)
    start = doc_start(ends, query)
    earliest = doc_start(ends, first + offset)
    latest = doc_start(ends, first + offset + width - 1)

    def one(step, masked):
        def part(columns):
            return jnp.concatenate(
                [ref[pl.ds(row, TOK), columns] for ref, row, base in step], axis=0
            )

        rows = TOK * len(step)

        def score(h):
            q = q_ref[pl.ds(offset, width), pl.ds(h * WIDTH, WIDTH)]
            return dot(part(pl.ds(0, WIDTH)), q, NT)

        if masked:
            inside = lax.broadcasted_iota(jnp.int32, (TOK, 1), 0)
            key = jnp.concatenate([base + inside for ref, row, base in step], axis=0)
            visible = key >= start
        wide = jnp.concatenate(
            [part(pl.ds(WIDTH, WIDTH)), jnp.ones((rows, EXTRA), BF16)], axis=1
        )
        scores = score(0)
        for h in range(HEADS):
            s = scores * SCALE
            if h + 1 < HEADS:
                scores = score(h + 1)
            if masked:
                s = jnp.where(visible, s, LOW)
            old = m_ref[h : h + 1, :]
            top = jnp.maximum(old, jnp.max(s, axis=0, keepdims=True))
            p = jnp.exp2(s - top).astype(BF16)
            m_ref[h : h + 1, :] = top
            acc_ref[h] = acc_ref[h] * jnp.exp2(old - top) + dot(wide, p, TN)

    for step in steps:
        highest = functools.reduce(jnp.maximum, [base for ref, row, base in step])
        lowest = functools.reduce(jnp.minimum, [base for ref, row, base in step])
        needed = (highest >= 0) & (highest + TOK > earliest)
        whole = (lowest >= 0) & (lowest >= latest)
        pl.when(needed & whole)(functools.partial(one, step, False))
        pl.when(needed & jnp.logical_not(whole))(functools.partial(one, step, True))


def place():
    ctx = lax.axis_index("ctx")
    x = lax.rem(ctx, 4)
    return ctx, ctx - x, x


def z_kernel(len_ref, q_ref, one_ref, two_ref, mi_ref, ai_ref, m_ref, acc_ref):
    ctx, _, _ = place()
    step = [(one_ref, 0, (ctx - 4) * TOK), (two_ref, 0, (ctx - 8) * TOK)]
    attend(q_ref, [step], doc_ends(len_ref), ctx * TOK, 0, TOK, m_ref, acc_ref)


def bases(row, x, other):
    return jnp.where(other < x, row + other, row - 8 + other) * TOK, (row - 4 + other) * TOK


def near_kernel(len_ref, q_ref, a_ref, b_ref, mi_ref, ai_ref, m_ref, acc_ref):
    ctx, row, x = place()
    steps = []
    for ref, other in ((a_ref, lax.bitwise_xor(x, 1)), (b_ref, 3 - x)):
        chosen, upper = bases(row, x, other)
        steps.append([(ref, 0, chosen), (ref, TOK, upper)])
    attend(q_ref, steps, doc_ends(len_ref), ctx * TOK, 0, TOK, m_ref, acc_ref)


def last_kernel(
    offset, len_ref, q_ref, a_ref, b_ref, mi_ref, ai_ref, c_ref, row_ref, inner_ref, before_ref, one_ref, two_ref, gap_ref, m_ref, acc_ref
):
    ctx, row, x = place()
    first = ctx * TOK
    ends = doc_ends(len_ref)
    now = pl.ds(offset, PART)
    m_ref[...] = mi_ref[:, now]
    acc_ref[...] = ai_ref[:, :, now]
    chosen, upper = bases(row, x, lax.bitwise_xor(x, 2))
    step = [(a_ref, 0, chosen), (b_ref, 0, upper)]
    attend(q_ref, [step], ends, first, offset, PART, m_ref, acc_ref)
    query = first + offset + lax.broadcasted_iota(jnp.int32, (1, PART), 1)
    enters = doc_start(ends, query) < first
    lane = lax.broadcasted_iota(jnp.int32, (PART, 128), 1)

    def enter(h):
        value, factor = pl.ds(h * STATE, STATE), pl.ds(256 + 8 * h, 1)
        above = jnp.where(ctx >= 8, two_ref[value, :], 0.0)
        above = jnp.where(ctx >= 4, one_ref[value, :] + one_ref[factor, :] * above, 0.0)
        return before_ref[value, :] + before_ref[factor, :] * above

    for h in range(HEADS):
        pair = pl.ds((h // 2) * 128, 128)
        mine = (lane < STATE) if h % 2 == 0 else (lane >= STATE)
        chosen = jnp.where(mine, c_ref[now, pair].astype(F32), 0.0).astype(BF16)
        entering = jnp.concatenate([enter(2 * (h // 2)), enter(2 * (h // 2) + 1)], axis=0)
        high = entering.astype(BF16)
        low = (entering - high.astype(F32)).astype(BF16)
        outer = dot(high, chosen, (((0,), (1,)), ((), ()))) + dot(
            low, chosen, (((0,), (1,)), ((), ()))
        )
        gate = jnp.where(enters, jnp.exp(row_ref[h : h + 1, now]), 0.0)
        student = inner_ref[pl.ds(h * WIDTH, WIDTH), now] + outer * gate
        teacher = acc_ref[h, :WIDTH, :] / acc_ref[h, WIDTH : WIDTH + 1, :]
        gap_ref[pl.ds(h * WIDTH, WIDTH), :] = (student - teacher).astype(BF16)


def project_kernel(w_ref, ws_ref, gap_ref, gs_ref, own_ref, up_ref, down_ref, far_ref):
    head = lax.axis_index("head")
    y, core = lax.div(head, 2), lax.rem(head, 2)
    for ref, step in ((far_ref, 2), (up_ref, 1), (down_ref, 3), (own_ref, 0)):
        to = lax.rem(y + step, 4)
        mine = pl.ds(pl.multiple_of((2 * to + core) * TOK, TOK), TOK)
        theirs = pl.ds(pl.multiple_of(to * TOK, TOK), TOK)
        total = dot(w_ref[:, mine], gap_ref[...], TN) + dot(ws_ref[:, theirs], gs_ref[...], TN)
        ref[...] = total.astype(ref.dtype)


def sum_kernel(*refs):
    out_ref, total_ref, sems = refs[-3:]
    copies = []
    for i in range(4):
        rows = pl.ds(i * 128, 128)
        for part in range(TOK // PART):
            own, up, down, far = (ref[rows, :].astype(F32) for ref in refs[4 * part : 4 * part + 4])
            total_ref[rows, pl.ds(part * PART, PART)] = (own + up) + (down + far)
        copies.append(
            pltpu.make_async_copy(total_ref.at[rows, :], out_ref.at[rows, :], sems.at[i])
        )
        copies[-1].start()
    for copy in copies:
        copy.wait()


def call(body, outs, name, ins, aliases=None, flops=0, scratch=(), out_specs=None, limit=24):
    return pl.pallas_call(
        body,
        out_shape=[jax.ShapeDtypeStruct(shape, kind) for shape, kind in outs],
        in_specs=ins,
        out_specs=out_specs or [VMEM] * len(outs),
        scratch_shapes=list(scratch),
        input_output_aliases=aliases or {},
        compiler_params=pltpu.CompilerParams(vmem_limit_bytes=limit << 20),
        cost_estimate=pl.CostEstimate(flops=flops, bytes_accessed=1024, transcendentals=0),
        name=name,
    )


def within(rows, pairs):
    return [(4 * z + a, 4 * z + b) for z in range(rows) for a, b in pairs]


def local(queries, key_rows, value_rows, b_input, c_input, step_log, lengths, out_weight):
    ctx = lax.axis_index("ctx")
    x = lax.rem(ctx, 4)
    even = within(4, [(0, 1), (1, 0), (2, 3), (3, 2)])
    odd = within(4, [(1, 2), (2, 1), (3, 0), (0, 3)])
    far = within(4, [(0, 2), (2, 0), (1, 3), (3, 1)])
    row_1 = [(i, (i + 4) % 16) for i in range(16)]
    row_2 = [(i, (i + 8) % 16) for i in range(16)]
    siblings = [(i, i ^ 1) for i in range(8)]

    sem = pltpu.SemaphoreType.DMA
    kv, state, cum_row, cum_col = call(
        state_kernel,
        [((TOK, 256), BF16), ((288, 128), F32), ((8, TOK), F32), ((TOK, 128), F32)],
        "shard_state",
        [SMEM] + [HBM] * 4,
        flops=2 << 30,
        scratch=[pltpu.VMEM((TOK, 256), BF16), pltpu.VMEM((HEADS, TOK), F32), sem((4,))],
        limit=54,
    )(lengths, key_rows, value_rows, step_log.T, b_input)
    kv_1 = lax.ppermute(kv, "ctx", row_1)
    kv_2 = lax.ppermute(kv, "ctx", row_2)
    m, acc, inner, q, c, for_sibling = call(
        own_kernel,
        [
            ((8, TOK), F32),
            ((HEADS, WIDTH + EXTRA, TOK), F32),
            ((TOK, TOK), F32),
            ((TOK, TOK), BF16),
            ((TOK, 256), BF16),
            ((TOK, 4 * TOK), BF16),
        ],
        "own_shard",
        [SMEM] + [VMEM] * 2 + [HBM] * 5,
        flops=6 << 30,
        scratch=[pltpu.VMEM((TOK, 256), BF16), pltpu.VMEM((TOK, 256), BF16), pltpu.VMEM((TOK, 8 * TOK), BF16), sem((12,))],
        out_specs=[VMEM] * 5 + [HBM],
        limit=54,
    )(lengths, cum_row, cum_col, kv, b_input, queries, c_input, out_weight)
    def split(packed):
        return packed[:256].reshape(HEADS, STATE, WIDTH), packed[256:].reshape(HEADS, 8, WIDTH)

    def pack(value, factor):
        return jnp.concatenate([value.reshape(256, WIDTH), factor.reshape(32, WIDTH)], axis=0)

    def join(earlier, later):
        return later[1][:, :1] * earlier[0] + later[0], earlier[1] * later[1]

    def choose(condition, yes, no):
        return tuple(jnp.where(condition, a, b) for a, b in zip(yes, no))

    mine = split(state)
    other = split(lax.ppermute(state, "ctx", even))
    is_odd, is_high = lax.rem(x, 2) == 1, x >= 2
    pair = join(choose(is_odd, other, mine), choose(is_odd, mine, other))
    none = (jnp.zeros_like(mine[0]), jnp.ones_like(mine[1]))
    before = choose(is_odd, other, none)

    other_pair = split(lax.ppermute(pack(*pair), "ctx", far))
    total = join(choose(is_high, other_pair, pair), choose(is_high, pair, other_pair))
    before = choose(is_high, join(other_pair, before), before)

    send_a = jnp.concatenate([jnp.where(lax.rem(x, 2) == 0, kv, kv_2), kv_1], axis=0)
    send_b = jnp.concatenate([jnp.where(x < 2, kv, kv_2), kv_1], axis=0)
    got_a = lax.ppermute(send_a, "ctx", even)
    got_b = lax.ppermute(send_b, "ctx", odd)

    m, acc = call(
        z_kernel,
        [((8, TOK), F32), ((HEADS, WIDTH + EXTRA, TOK), F32)],
        "same_column",
        [SMEM] + [VMEM] * 5,
        aliases={4: 0, 5: 1},
        flops=4 << 30,
    )(lengths, q, kv_1, kv_2, m, acc)

    packed_total = pack(*total)
    w_sibling = lax.ppermute(for_sibling, "head", siblings)
    total_1 = lax.ppermute(packed_total, "ctx", row_1)
    total_2 = lax.ppermute(packed_total, "ctx", row_2)
    before = pack(*before)

    far_a = lax.ppermute(got_b[:TOK], "ctx", even)
    far_b = lax.ppermute(got_a[TOK:], "ctx", odd)

    m, acc = call(
        near_kernel,
        [((8, TOK), F32), ((HEADS, WIDTH + EXTRA, TOK), F32)],
        "near_columns",
        [SMEM] + [VMEM] * 5,
        aliases={4: 0, 5: 1},
        flops=7 << 30,
    )(lengths, q, got_a, got_b, m, acc)

    def line(step):
        return [(2 * y + c, 2 * ((y + step) % 4) + c) for y in range(4) for c in range(2)]

    pieces = []
    for part in range(TOK // PART):
        (gap,) = call(
            functools.partial(last_kernel, part * PART),
            [((TOK, PART), BF16)],
            "far_column",
            [SMEM] + [VMEM] * 11,
            flops=5 << 29,
            scratch=[pltpu.VMEM((8, PART), F32), pltpu.VMEM((HEADS, WIDTH + EXTRA, PART), F32)],
        )(lengths, q, far_a, far_b, m, acc, c, cum_row, inner, before, total_1, total_2)
        gap_sibling = lax.ppermute(gap, "head", siblings)
        own, up, down, opposite = call(
            project_kernel,
            [((TOK, PART), F32)] + [((TOK, PART), BF16)] * 3,
            "project",
            [VMEM] * 4,
            flops=3 << 29,
        )(out_weight, w_sibling, gap, gap_sibling)
        opposite = lax.ppermute(opposite, "head", line(2))
        up = lax.ppermute(up, "head", line(1))
        down = lax.ppermute(down, "head", line(3))
        pieces += [own, up, down, opposite]
    (result,) = call(
        sum_kernel,
        [((TOK, TOK), F32)],
        "sum_line",
        [VMEM] * len(pieces),
        flops=1024,
        scratch=[pltpu.VMEM((TOK, TOK), F32), pltpu.SemaphoreType.DMA((4,))],
        out_specs=[HBM],
    )(*pieces)
    return result


def solution(mesh):
    split = P("ctx", "head")
    in_specs = (split, split, split, split, split, split, P(), P("head", None))
    return jax.shard_map(
        local, mesh=mesh, in_specs=in_specs, out_specs=P("head", "ctx"), check_vma=False
    )
```

```python
import functools

import jax
import jax.numpy as jnp
from jax import lax
from jax.experimental import pallas as pl
from jax.experimental.pallas import tpu as pltpu
from jax.sharding import PartitionSpec as P

TOK = 512
HEADS = 4
WIDTH = 128
STATE = 64
EXTRA = 16
SCALE = WIDTH**-0.5 * 1.4426950408889634
LOW = -1e30
NT = (((1,), (1,)), ((), ()))
TN = (((0,), (0,)), ((), ()))
F32 = jnp.float32
BF16 = jnp.bfloat16
VMEM = pl.BlockSpec(memory_space=pltpu.VMEM)
SMEM = pl.BlockSpec(memory_space=pltpu.SMEM)
HBM = pl.BlockSpec(memory_space=pltpu.HBM)
PART = 256


def dot(a, b, dims):
    return lax.dot_general(a, b, dims, preferred_element_type=F32)


def doc_ends(len_ref):
    ends, total = [], jnp.int32(0)
    for d in range(7):
        total = total + len_ref[d]
        ends.append(total)
    return ends


def doc_start(ends, position):
    start = jnp.zeros_like(position)
    for end in ends:
        start = jnp.where(position >= end, end, start)
    return start


def three(value):
    one = value.astype(BF16)
    rest = value - one.astype(F32)
    two = rest.astype(BF16)
    return one, two, (rest - two.astype(F32)).astype(BF16)


def begin(pairs, sems, first=0):
    copies = [pltpu.make_async_copy(a, b, sems.at[first + i]) for i, (a, b) in enumerate(pairs)]
    for copy in copies:
        copy.start()
    return copies


def running_sums(log):
    tri = (
        lax.broadcasted_iota(jnp.int32, (TOK, TOK), 0)
        >= lax.broadcasted_iota(jnp.int32, (TOK, TOK), 1)
    ).astype(F32).astype(BF16)
    parts = three(log)
    col = sum(dot(tri, part, NT) for part in parts[::-1])
    row = sum(dot(part, tri, NT) for part in parts[::-1])
    return col, row


def shard_state(first, last_start, b_ref, v, col, st_ref):
    final = col[TOK - 1 :, :]
    where_now = first + lax.broadcasted_iota(jnp.int32, (TOK, HEADS), 0)
    weight = jnp.exp(jnp.where(where_now >= last_start, final - col, -jnp.inf))
    lane = lax.broadcasted_iota(jnp.int32, (TOK, 128), 1)
    for pair in range(2):
        spread = jnp.where(
            lane < STATE,
            jnp.broadcast_to(weight[:, 2 * pair : 2 * pair + 1], (TOK, 128)),
            jnp.broadcast_to(weight[:, 2 * pair + 1 : 2 * pair + 2], (TOK, 128)),
        )
        scaled = b_ref[:, pl.ds(pair * 128, 128)].astype(F32) * spread
        high = scaled.astype(BF16)
        low = (scaled - high.astype(F32)).astype(BF16)
        st_ref[pl.ds(pair * 128, 128), :] = dot(high, v, TN) + dot(low, v, TN)
    kept = jnp.where(last_start < first, 1.0, 0.0).astype(F32)
    for h in range(HEADS):
        st_ref[pl.ds(256 + 8 * h, 8), :] = jnp.broadcast_to(
            jnp.exp(final[:, h : h + 1]) * kept, (8, 128)
        )


def state_kernel(
    len_ref, k_any, v_any, log_any, b_any, kv_ref, st_ref, row_ref, col_ref, b_ref, log_ref, sems
):
    pairs = (
        (log_any, log_ref),
        (v_any, kv_ref.at[:, pl.ds(WIDTH, WIDTH)]),
        (b_any, b_ref),
        (k_any, kv_ref.at[:, pl.ds(0, WIDTH)]),
    )
    logs, values, inputs, keys = begin(pairs, sems)
    logs.wait()
    col, row = running_sums(log_ref[...])
    for copy in (values, inputs, keys):
        copy.wait()
    first = lax.axis_index("ctx") * TOK
    last_start = doc_start(doc_ends(len_ref), first + TOK - 1)
    shard_state(first, last_start, b_ref, kv_ref[:, WIDTH:], col, st_ref)
    row_ref[...] = jnp.concatenate([row, jnp.zeros((8 - HEADS, TOK), F32)], axis=0)
    col_ref[...] = jnp.concatenate([col, jnp.zeros((TOK, 128 - HEADS), F32)], axis=1)


def own_kernel(
    len_ref,
    row_ref,
    col_ref,
    kv_any,
    b_any,
    q_any,
    c_any,
    w_any,
    m_ref,
    acc_ref,
    inner_ref,
    q_ref,
    c_ref,
    send_ref,
    kv_ref,
    b_ref,
    w_ref,
    sems,
):
    pairs = ((q_any, q_ref), (kv_any, kv_ref), (b_any, b_ref), (c_any, c_ref))
    for copy in begin(pairs, sems):
        copy.wait()
    other = 1 - lax.rem(lax.axis_index("head"), 2)
    loads, cuts = [], []
    for j in range(4):
        rows = pl.ds(j * 128, 128)
        loads.append((w_any.at[rows, :], w_ref.at[rows, :]))
        source = pl.ds(pl.multiple_of((2 * j + other) * TOK, TOK), TOK)
        cuts.append((w_ref.at[:, source], send_ref.at[:, pl.ds(j * TOK, TOK)]))
    loads = begin(loads, sems, 4)
    first = lax.axis_index("ctx") * TOK
    ends = doc_ends(len_ref)
    v = kv_ref[:, WIDTH:]
    query = first + lax.broadcasted_iota(jnp.int32, (1, TOK), 1)
    start = doc_start(ends, query)
    key = first + lax.broadcasted_iota(jnp.int32, (TOK, 1), 0)
    v = kv_ref[:, WIDTH:]
    wide = jnp.concatenate([v, jnp.ones((TOK, EXTRA), BF16)], axis=1)
    lane = lax.broadcasted_iota(jnp.int32, (PART, 128), 1)
    units = [(h, half) for h in range(HEADS) for half in range(TOK // PART)]

    def score(h, half):
        q = q_ref[pl.ds(half * PART, PART), pl.ds(h * WIDTH, WIDTH)]
        return dot(kv_ref[pl.ds(0, (half + 1) * PART), :WIDTH], q, NT)

    def products(h, half):
        pair = pl.ds((h // 2) * 128, 128)
        mine = (lane < STATE) if h % 2 == 0 else (lane >= STATE)
        c = c_ref[pl.ds(half * PART, PART), pair].astype(F32)
        chosen = jnp.where(mine, c, 0.0).astype(BF16)
        return dot(b_ref[pl.ds(0, (half + 1) * PART), pair], chosen, NT)

    scores = score(*units[0])
    for i, (h, half) in enumerate(units):
        if h == 2 and half == 0:
            for copy in loads:
                copy.wait()
            cuts = begin(cuts, sems, 8)
        now, until = pl.ds(half * PART, PART), (half + 1) * PART
        columns = slice(half * PART, until)
        visible = (key[:until] >= start[:, columns]) & (key[:until] <= query[:, columns])
        mixed = products(h, half)
        s = jnp.where(visible, scores * SCALE, LOW)
        top = jnp.max(s, axis=0, keepdims=True)
        p = jnp.exp2(s - top).astype(BF16)
        if i + 1 < len(units):
            scores = score(*units[i + 1])
        m_ref[h : h + 1, now] = top
        acc_ref[h, :, now] = dot(wide[:until], p, TN)
        gap = row_ref[h : h + 1, now] - col_ref[pl.ds(0, until), h : h + 1]
        mixing = (mixed * jnp.exp(jnp.where(visible, gap, -jnp.inf))).astype(BF16)
        inner_ref[pl.ds(h * WIDTH, WIDTH), now] = dot(v[:until], mixing, TN)
    m_ref[HEADS:, :] = jnp.zeros((8 - HEADS, TOK), F32)
    for copy in cuts:
        copy.wait()


def attend(q_ref, steps, ends, first, offset, width, m_ref, acc_ref):
    query = first + offset + lax.broadcasted_iota(jnp.int32, (1, width), 1)
    start = doc_start(ends, query)
    earliest = doc_start(ends, first + offset)
    latest = doc_start(ends, first + offset + width - 1)

    def one(step, masked):
        def part(columns):
            return jnp.concatenate(
                [ref[pl.ds(row, TOK), columns] for ref, row, base in step], axis=0
            )

        rows = TOK * len(step)

        def score(h):
            q = q_ref[pl.ds(offset, width), pl.ds(h * WIDTH, WIDTH)]
            return dot(part(pl.ds(0, WIDTH)), q, NT)

        if masked:
            inside = lax.broadcasted_iota(jnp.int32, (TOK, 1), 0)
            key = jnp.concatenate([base + inside for ref, row, base in step], axis=0)
            visible = key >= start
        wide = jnp.concatenate(
            [part(pl.ds(WIDTH, WIDTH)), jnp.ones((rows, EXTRA), BF16)], axis=1
        )
        scores = score(0)
        for h in range(HEADS):
            s = scores * SCALE
            if h + 1 < HEADS:
                scores = score(h + 1)
            if masked:
                s = jnp.where(visible, s, LOW)
            old = m_ref[h : h + 1, :]
            top = jnp.maximum(old, jnp.max(s, axis=0, keepdims=True))
            p = jnp.exp2(s - top).astype(BF16)
            m_ref[h : h + 1, :] = top
            acc_ref[h] = acc_ref[h] * jnp.exp2(old - top) + dot(wide, p, TN)

    for step in steps:
        highest = functools.reduce(jnp.maximum, [base for ref, row, base in step])
        lowest = functools.reduce(jnp.minimum, [base for ref, row, base in step])
        needed = (highest >= 0) & (highest + TOK > earliest)
        whole = (lowest >= 0) & (lowest >= latest)
        pl.when(needed & whole)(functools.partial(one, step, False))
        pl.when(needed & jnp.logical_not(whole))(functools.partial(one, step, True))


def place():
    ctx = lax.axis_index("ctx")
    x = lax.rem(ctx, 4)
    return ctx, ctx - x, x


def z_kernel(len_ref, q_ref, one_ref, two_ref, mi_ref, ai_ref, m_ref, acc_ref):
    ctx, _, _ = place()
    step = [(one_ref, 0, (ctx - 4) * TOK), (two_ref, 0, (ctx - 8) * TOK)]
    attend(q_ref, [step], doc_ends(len_ref), ctx * TOK, 0, TOK, m_ref, acc_ref)


def bases(row, x, other):
    return jnp.where(other < x, row + other, row - 8 + other) * TOK, (row - 4 + other) * TOK


def near_kernel(len_ref, q_ref, a_ref, b_ref, mi_ref, ai_ref, m_ref, acc_ref):
    ctx, row, x = place()
    steps = []
    for ref, other in ((a_ref, lax.bitwise_xor(x, 1)), (b_ref, 3 - x)):
        chosen, upper = bases(row, x, other)
        steps.append([(ref, 0, chosen), (ref, TOK, upper)])
    attend(q_ref, steps, doc_ends(len_ref), ctx * TOK, 0, TOK, m_ref, acc_ref)


def last_kernel(
    offset, len_ref, q_ref, a_ref, b_ref, mi_ref, ai_ref, c_ref, row_ref, inner_ref, before_ref, one_ref, two_ref, gap_ref, m_ref, acc_ref
):
    ctx, row, x = place()
    first = ctx * TOK
    ends = doc_ends(len_ref)
    now = pl.ds(offset, PART)
    m_ref[...] = mi_ref[:, now]
    acc_ref[...] = ai_ref[:, :, now]
    chosen, upper = bases(row, x, lax.bitwise_xor(x, 2))
    step = [(a_ref, 0, chosen), (b_ref, 0, upper)]
    attend(q_ref, [step], ends, first, offset, PART, m_ref, acc_ref)
    query = first + offset + lax.broadcasted_iota(jnp.int32, (1, PART), 1)
    enters = doc_start(ends, query) < first
    lane = lax.broadcasted_iota(jnp.int32, (PART, 128), 1)

    def enter(h):
        value, factor = pl.ds(h * STATE, STATE), pl.ds(256 + 8 * h, 1)
        above = jnp.where(ctx >= 8, two_ref[value, :], 0.0)
        above = jnp.where(ctx >= 4, one_ref[value, :] + one_ref[factor, :] * above, 0.0)
        return before_ref[value, :] + before_ref[factor, :] * above

    for h in range(HEADS):
        pair = pl.ds((h // 2) * 128, 128)
        mine = (lane < STATE) if h % 2 == 0 else (lane >= STATE)
        chosen = jnp.where(mine, c_ref[now, pair].astype(F32), 0.0).astype(BF16)
        entering = jnp.concatenate([enter(2 * (h // 2)), enter(2 * (h // 2) + 1)], axis=0)
        high = entering.astype(BF16)
        low = (entering - high.astype(F32)).astype(BF16)
        outer = dot(high, chosen, (((0,), (1,)), ((), ()))) + dot(
            low, chosen, (((0,), (1,)), ((), ()))
        )
        gate = jnp.where(enters, jnp.exp(row_ref[h : h + 1, now]), 0.0)
        student = inner_ref[pl.ds(h * WIDTH, WIDTH), now] + outer * gate
        teacher = acc_ref[h, :WIDTH, :] / acc_ref[h, WIDTH : WIDTH + 1, :]
        gap_ref[pl.ds(h * WIDTH, WIDTH), :] = (student - teacher).astype(BF16)


def project_kernel(w_ref, ws_ref, gap_ref, gs_ref, own_ref, up_ref, down_ref, far_ref):
    head = lax.axis_index("head")
    y, core = lax.div(head, 2), lax.rem(head, 2)
    for ref, step in ((far_ref, 2), (up_ref, 1), (down_ref, 3), (own_ref, 0)):
        to = lax.rem(y + step, 4)
        mine = pl.ds(pl.multiple_of((2 * to + core) * TOK, TOK), TOK)
        theirs = pl.ds(pl.multiple_of(to * TOK, TOK), TOK)
        total = dot(w_ref[:, mine], gap_ref[...], TN) + dot(ws_ref[:, theirs], gs_ref[...], TN)
        ref[...] = total.astype(ref.dtype)


def sum_kernel(*refs):
    out_ref, total_ref, sems = refs[-3:]
    copies = []
    for i in range(4):
        rows = pl.ds(i * 128, 128)
        for part in range(TOK // PART):
            own, up, down, far = (ref[rows, :].astype(F32) for ref in refs[4 * part : 4 * part + 4])
            total_ref[rows, pl.ds(part * PART, PART)] = (own + up) + (down + far)
        copies.append(
            pltpu.make_async_copy(total_ref.at[rows, :], out_ref.at[rows, :], sems.at[i])
        )
        copies[-1].start()
    for copy in copies:
        copy.wait()


def call(body, outs, name, ins, aliases=None, flops=0, scratch=(), out_specs=None, limit=24):
    return pl.pallas_call(
        body,
        out_shape=[jax.ShapeDtypeStruct(shape, kind) for shape, kind in outs],
        in_specs=ins,
        out_specs=out_specs or [VMEM] * len(outs),
        scratch_shapes=list(scratch),
        input_output_aliases=aliases or {},
        compiler_params=pltpu.CompilerParams(vmem_limit_bytes=limit << 20),
        cost_estimate=pl.CostEstimate(flops=flops, bytes_accessed=1024, transcendentals=0),
        name=name,
    )


def within(rows, pairs):
    return [(4 * z + a, 4 * z + b) for z in range(rows) for a, b in pairs]


def local(queries, key_rows, value_rows, b_input, c_input, step_log, lengths, out_weight):
    ctx = lax.axis_index("ctx")
    x = lax.rem(ctx, 4)
    even = within(4, [(0, 1), (1, 0), (2, 3), (3, 2)])
    odd = within(4, [(1, 2), (2, 1), (3, 0), (0, 3)])
    far = within(4, [(0, 2), (2, 0), (1, 3), (3, 1)])
    row_1 = [(i, (i + 4) % 16) for i in range(16)]
    row_2 = [(i, (i + 8) % 16) for i in range(16)]
    siblings = [(i, i ^ 1) for i in range(8)]

    sem = pltpu.SemaphoreType.DMA
    kv, state, cum_row, cum_col = call(
        state_kernel,
        [((TOK, 256), BF16), ((288, 128), F32), ((8, TOK), F32), ((TOK, 128), F32)],
        "shard_state",
        [SMEM] + [HBM] * 4,
        flops=2 << 30,
        scratch=[pltpu.VMEM((TOK, 256), BF16), pltpu.VMEM((HEADS, TOK), F32), sem((4,))],
        limit=54,
    )(lengths, key_rows, value_rows, step_log.T, b_input)
    kv_1 = lax.ppermute(kv, "ctx", row_1)
    kv_2 = lax.ppermute(kv, "ctx", row_2)
    m, acc, inner, q, c, for_sibling = call(
        own_kernel,
        [
            ((8, TOK), F32),
            ((HEADS, WIDTH + EXTRA, TOK), F32),
            ((TOK, TOK), F32),
            ((TOK, TOK), BF16),
            ((TOK, 256), BF16),
            ((TOK, 4 * TOK), BF16),
        ],
        "own_shard",
        [SMEM] + [VMEM] * 2 + [HBM] * 5,
        flops=6 << 30,
        scratch=[pltpu.VMEM((TOK, 256), BF16), pltpu.VMEM((TOK, 256), BF16), pltpu.VMEM((TOK, 8 * TOK), BF16), sem((12,))],
        out_specs=[VMEM] * 5 + [HBM],
        limit=54,
    )(lengths, cum_row, cum_col, kv, b_input, queries, c_input, out_weight)
    def split(packed):
        return packed[:256].reshape(HEADS, STATE, WIDTH), packed[256:].reshape(HEADS, 8, WIDTH)

    def pack(value, factor):
        return jnp.concatenate([value.reshape(256, WIDTH), factor.reshape(32, WIDTH)], axis=0)

    def join(earlier, later):
        return later[1][:, :1] * earlier[0] + later[0], earlier[1] * later[1]

    def choose(condition, yes, no):
        return tuple(jnp.where(condition, a, b) for a, b in zip(yes, no))

    mine = split(state)
    other = split(lax.ppermute(state, "ctx", even))
    is_odd, is_high = lax.rem(x, 2) == 1, x >= 2
    pair = join(choose(is_odd, other, mine), choose(is_odd, mine, other))
    none = (jnp.zeros_like(mine[0]), jnp.ones_like(mine[1]))
    before = choose(is_odd, other, none)

    other_pair = split(lax.ppermute(pack(*pair), "ctx", far))
    total = join(choose(is_high, other_pair, pair), choose(is_high, pair, other_pair))
    before = choose(is_high, join(other_pair, before), before)

    send_a = jnp.concatenate([jnp.where(lax.rem(x, 2) == 0, kv, kv_2), kv_1], axis=0)
    send_b = jnp.concatenate([jnp.where(x < 2, kv, kv_2), kv_1], axis=0)
    got_a = lax.ppermute(send_a, "ctx", even)
    got_b = lax.ppermute(send_b, "ctx", odd)

    m, acc = call(
        z_kernel,
        [((8, TOK), F32), ((HEADS, WIDTH + EXTRA, TOK), F32)],
        "same_column",
        [SMEM] + [VMEM] * 5,
        aliases={4: 0, 5: 1},
        flops=4 << 30,
    )(lengths, q, kv_1, kv_2, m, acc)

    packed_total = pack(*total)
    w_sibling = lax.ppermute(for_sibling, "head", siblings)
    total_1 = lax.ppermute(packed_total, "ctx", row_1)
    total_2 = lax.ppermute(packed_total, "ctx", row_2)
    before = pack(*before)

    far_a = lax.ppermute(got_b[:TOK], "ctx", even)
    far_b = lax.ppermute(got_a[TOK:], "ctx", odd)

    m, acc = call(
        near_kernel,
        [((8, TOK), F32), ((HEADS, WIDTH + EXTRA, TOK), F32)],
        "near_columns",
        [SMEM] + [VMEM] * 5,
        aliases={4: 0, 5: 1},
        flops=7 << 30,
    )(lengths, q, got_a, got_b, m, acc)

    def line(step):
        return [(2 * y + c, 2 * ((y + step) % 4) + c) for y in range(4) for c in range(2)]

    pieces = []
    for part in range(TOK // PART):
        (gap,) = call(
            functools.partial(last_kernel, part * PART),
            [((TOK, PART), BF16)],
            "far_column",
            [SMEM] + [VMEM] * 11,
            flops=5 << 29,
            scratch=[pltpu.VMEM((8, PART), F32), pltpu.VMEM((HEADS, WIDTH + EXTRA, PART), F32)],
        )(lengths, q, far_a, far_b, m, acc, c, cum_row, inner, before, total_1, total_2)
        gap_sibling = lax.ppermute(gap, "head", siblings)
        own, up, down, opposite = call(
            project_kernel,
            [((TOK, PART), F32)] + [((TOK, PART), BF16)] * 3,
            "project",
            [VMEM] * 4,
            flops=3 << 29,
        )(out_weight, w_sibling, gap, gap_sibling)
        opposite = lax.ppermute(opposite, "head", line(2))
        up = lax.ppermute(up, "head", line(1))
        down = lax.ppermute(down, "head", line(3))
        pieces += [own, up, down, opposite]
    (result,) = call(
        sum_kernel,
        [((TOK, TOK), F32)],
        "sum_line",
        [VMEM] * len(pieces),
        flops=1024,
        scratch=[pltpu.VMEM((TOK, TOK), F32), pltpu.SemaphoreType.DMA((4,))],
        out_specs=[HBM],
    )(*pieces)
    return result


def solution(mesh):
    split = P("ctx", "head")
    in_specs = (split, split, split, split, split, split, P(), P("head", None))
    return jax.shard_map(
        local, mesh=mesh, in_specs=in_specs, out_specs=P("head", "ctx"), check_vma=False
    )
```
